1024 devices in a mesh: gx: 32 (over z), gy: 4 (over x), gz: 8 (over y, core).
Axes of the slice: x: 4, y: 4, z: 32, core: 2. Of those that a mesh axis runs over, the one named last changes fastest.
Arguments:
- charges: float32 [256, 4, 8, 512], P('gx', 'gy', 'gz'), may hold values from -3 to 3
- offsets: float32 [3, 256, 4, 8, 512], P(None, 'gx', 'gy', 'gz'), may hold values from 0 to 1
- cells: int32 [2, 256, 4, 8, 512], P(None, 'gx', 'gy', 'gz'), may hold values from 0 to 1023, as said below
- kernel: bfloat16 [17, 17, 17], replicated, may hold values from -0.078125 to 0.078125
Outputs:
- potential: float32 [256, 32, 1024], P('gx', 'gy', 'gz')
- forces: float32 [3, 256, 4, 8, 512], P(None, 'gx', 'gy', 'gz')
The draws below stay inside these ranges and needn't reach their ends.
Inputs may be any that keep to these rules, and one draw needn't show every extreme that they name: cells[0] lies in the block of 8 rows that belongs to the atom's second index (index g: g * 8 to g * 8 + 7); cells[1] lies likewise in the block of 128 that belongs to its third index.
All inputs are finite; a program needn't handle non-finite values.
Results may differ from the reference program's by a relative error of at most 0.0029.
Values may be sent and summed in bfloat16 or wider, within the bound.
A program may use at most 64 MiB of HBM per device.

```python
import jax
import jax.numpy as jnp
from jax import lax

CY = 8
CZ = 128
APT = 512
KSPAN = 17
NX = 256
NY = 32
NZ = 1024
N_GY = 4
N_GZ = 8


def draw_cells(key, part):
    key_y, key_z = jax.random.split(jax.random.fold_in(key, 17))
    array_shape = (NX, NY // CY, NZ // CZ, APT)
    local_y = jax.random.randint(key_y, array_shape, 0, CY, dtype=jnp.int32)
    local_z = jax.random.randint(key_z, array_shape, 0, CZ, dtype=jnp.int32)
    block_y = jnp.arange(NY // CY, dtype=jnp.int32)[None, :, None, None] * CY
    block_z = jnp.arange(NZ // CZ, dtype=jnp.int32)[None, None, :, None] * CZ
    return jnp.stack([local_y + block_y, local_z + block_z]).astype(jnp.int32)


def block_levels(stream_key, shape, shards, low, top_value):
    def one(dim, parts):
        draws = jax.random.uniform(jax.random.fold_in(jax.random.fold_in(stream_key, 6), dim), (parts,), jnp.float32, low / len(shards), top_value / len(shards))
        return jnp.repeat(jnp.exp(draws), shape[dim] // parts).reshape((-1,) + (1,) * (len(shape) - dim - 1))

    level = one(*shards[0])
    for cut in shards[1:]:
        level = level * one(*cut)
    return level


def normal_values(key, extent, deviation, bound, cuts=(), kind=jnp.bfloat16):
    result = deviation * jax.random.normal(key, extent, jnp.float32)
    if cuts:
        result = result * block_levels(key, extent, cuts, -0.22, 0.18)
    return jnp.clip(result, -bound, bound).astype(kind)


def setup_inputs(seed: int = 0) -> dict:
    arg_keys = jax.random.split(jax.random.key(seed), 5)
    return {
        "charges": normal_values(arg_keys[0], (NX, N_GY, N_GZ, APT), 0.5, 3.0, ((0, 32), (1, 4), (2, 8)), jnp.float32),
        "offsets": jnp.clip(1.0 * jax.random.uniform(arg_keys[1], (3, NX, N_GY, N_GZ, APT), jnp.float32) ** block_levels(arg_keys[1], (3, NX, N_GY, N_GZ, APT), ((1, 32), (2, 4), (3, 8)), -0.2, 0.2), 0.0, 1.0),
        "cells": draw_cells(jax.random.fold_in(arg_keys[4], 71), 0),
        "kernel": normal_values(arg_keys[3], (KSPAN, KSPAN, KSPAN), (KSPAN * KSPAN * KSPAN) ** -0.5, 0.078125),
    }


def spline(fraction):
    remain = 1.0 - fraction
    values = [remain ** 3 / 6.0,
              (3.0 * fraction ** 3 - 6.0 * fraction ** 2 + 4.0) / 6.0,
              (-3.0 * fraction ** 3 + 3.0 * fraction ** 2 + 3.0 * fraction + 1.0) / 6.0,
              fraction ** 3 / 6.0]
    slopes = [-0.5 * remain ** 2,
              1.5 * fraction ** 2 - 2.0 * fraction,
              -1.5 * fraction ** 2 + fraction + 0.5,
              0.5 * fraction ** 2]
    return values, slopes


def reference(charges, offsets, cells, kernel):
    plane = jnp.broadcast_to(jnp.arange(NX, dtype=jnp.int32)[:, None, None, None], charges.shape).reshape(-1)
    column_y = cells[0].reshape(-1)
    column_z = cells[1].reshape(-1)
    charge_flat = charges.reshape(-1)
    x_values, x_slopes = spline(offsets[0].reshape(-1))
    y_values, y_slopes = spline(offsets[1].reshape(-1))
    z_values, z_slopes = spline(offsets[2].reshape(-1))
    grid = jnp.zeros((NX * NY * NZ,), jnp.float32)
    for shift_a in range(4):
        for shift_b in range(4):
            row_index = ((plane + shift_a - 1) % NX) * NY + (column_y + shift_b - 1) % NY
            weight_ab = charge_flat * x_values[shift_a] * y_values[shift_b]
            for shift_c in range(4):
                target = (row_index * NZ + (column_z + shift_c - 1) % NZ).astype(jnp.int32)
                grid = grid.at[target].add(weight_ab * z_values[shift_c])
    rounded = lax.optimization_barrier(grid.reshape(NX, NY, NZ).astype(jnp.bfloat16)).astype(jnp.float32)
    radius = KSPAN // 2
    spots = radius - jnp.arange(KSPAN, dtype=jnp.int32)
    wrapped = jnp.zeros((NX, NY, NZ), jnp.float32).at[
        (spots % NX)[:, None, None], (spots % NY)[None, :, None], (spots % NZ)[None, None, :]
    ].add(kernel.astype(jnp.float32))
    potential = jnp.fft.irfftn(jnp.fft.rfftn(rounded) * jnp.fft.rfftn(wrapped), s=(NX, NY, NZ)).astype(jnp.float32)
    flat_potential = potential.reshape(-1)
    force_x = jnp.zeros_like(charge_flat)
    force_y = jnp.zeros_like(charge_flat)
    force_z = jnp.zeros_like(charge_flat)
    for shift_a in range(4):
        for shift_b in range(4):
            row_index = ((plane + shift_a - 1) % NX) * NY + (column_y + shift_b - 1) % NY
            for shift_c in range(4):
                target = (row_index * NZ + (column_z + shift_c - 1) % NZ).astype(jnp.int32)
                sample = flat_potential[target]
                force_x = force_x + x_slopes[shift_a] * y_values[shift_b] * z_values[shift_c] * sample
                force_y = force_y + x_values[shift_a] * y_slopes[shift_b] * z_values[shift_c] * sample
                force_z = force_z + x_values[shift_a] * y_values[shift_b] * z_slopes[shift_c] * sample
    forces = -charge_flat[None, :] * jnp.stack([force_x, force_y, force_z])
    return potential, forces.reshape(3, NX, N_GY, N_GZ, APT)
```

```python
import jax
import jax.numpy as jnp
from jax import lax
from jax.experimental import pallas as pl
from jax.experimental.pallas import tpu as pltpu
from jax.sharding import PartitionSpec as P

CX = 8
CY = 8
CZ = 128
TILES = 8
APT = 512
SPAN = 17
ZROWS = 160
MESH = pl.DeviceIdType.MESH

FOLD = [
    (dx, dy, dz)
    for dz in (1, -1, 0)
    for dx in (1, -1, 0)
    for dy in (1, -1, 0)
    if (dx, dy, dz) != (0, 0, 0)
]
HALO = [(dx, dy) for dx in (1, -1) for dy in (2, 1, -1, 0)]
HALO += [(dx, dy) for dx in (2, -2) for dy in (2, 1, -1, 0)]
HALO += [(0, dy) for dy in (2, 1, -1)]
PEERS = sorted({(dx, dy % 4, dz) for dx, dy, dz in FOLD} | {(dx, dy % 4, 0) for dx, dy in HALO})


def device_at(dx, dy, dz):
    where = []
    for axis, step in (("gx", dx), ("gy", dy), ("gz", dz)):
        size = lax.axis_size(axis)
        index = lax.axis_index(axis)
        where.append(lax.rem(index + (step + size), size) if step else index)
    return tuple(where)


def x_splines(f):
    r = 1.0 - f
    values = [
        r * r * r / 6.0,
        (3.0 * f * f * f - 6.0 * f * f + 4.0) / 6.0,
        (-3.0 * f * f * f + 3.0 * f * f + 3.0 * f + 1.0) / 6.0,
        f * f * f / 6.0,
    ]
    slopes = [-0.5 * r * r, 1.5 * f * f - 2.0 * f, -1.5 * f * f + f + 0.5, 0.5 * f * f]
    return values, slopes


def bspline(u):
    a = jnp.abs(u)
    p = jnp.maximum(2.0 - a, 0.0)
    q = jnp.maximum(1.0 - a, 0.0)
    return p * p * p * (1.0 / 6.0) - q * q * q * (2.0 / 3.0)


def bslope(u):
    a = jnp.abs(u)
    p = jnp.maximum(2.0 - a, 0.0)
    q = jnp.maximum(1.0 - a, 0.0)
    m = 0.5 * p * p - 2.0 * q * q
    return jnp.where(u < 0.0, -m, m)


def split(value):
    high = value.astype(jnp.bfloat16)
    low = (value - high.astype(jnp.float32)).astype(jnp.bfloat16)
    return high, low


def mm(a, b):
    return jnp.dot(a, b, preferred_element_type=jnp.float32)


def mm_nt(a, b):
    return lax.dot_general(a, b, (((1,), (1,)), ((), ())), preferred_element_type=jnp.float32)


def body(
    q_ref, off_ref, cell_ref, kern_ref, pot_ref, frc_ref,
    zrow, zwh, zwl, zsh, zsl, pm, pe, zbuf, sbuf, rz, r0, fm, hb, rh,
    xf, tf, tb, w, phh, phl, send1, recv1, send2, recv2,
):
    iy = lax.axis_index("gy")
    iz = lax.axis_index("gz")
    f32, bf16 = jnp.float32, jnp.bfloat16

    barrier = pltpu.get_barrier_semaphore()
    for peer in PEERS:
        pl.semaphore_signal(barrier, inc=1, device_id=device_at(*peer), device_id_type=MESH)

    row_id = lax.broadcasted_iota(jnp.int32, (ZROWS, 128), 0)
    zrow[...] = jnp.where(
        row_id < 128, row_id, jnp.where(row_id < 144, row_id - 9, row_id - 145)
    ).astype(f32)
    pm[...] = jnp.zeros_like(pm)
    pe[...] = jnp.zeros_like(pe)
    y_id = lax.broadcasted_iota(jnp.int32, (16, APT), 0)
    y_id = jnp.where(y_id < 15, y_id, -1).astype(f32)

    def y_distance(t):
        ly = (cell_ref[0, t, 0] - iy * CY).astype(f32)
        return (y_id - ly) - off_ref[1, t, 0]

    def z_position(t):
        return (cell_ref[1, t, 0] - iz * CZ).astype(f32) + off_ref[2, t, 0]

    def spread(t, carry):
        zpos = z_position(t)
        for c in range(ZROWS // 16):
            zz = zrow[pl.ds(16 * c, 16), :]
            u = jnp.concatenate([zz] * 4, axis=1) - zpos
            high, low = split(bspline(u))
            zwh[t, pl.ds(16 * c, 16), :] = high
            zwl[t, pl.ds(16 * c, 16), :] = low
        wy = bspline(y_distance(t))
        wx, _ = x_splines(off_ref[0, t, 0])
        charge = q_ref[t, 0]
        parts = [split((charge * wx[k]) * wy) for k in range(4)]
        high = jnp.concatenate([p[0] for p in parts], axis=0)
        both = jnp.concatenate([high] + [p[1] for p in parts], axis=0)
        first = mm_nt(both, zwh[t])
        total = first[:64] + first[64:] + mm_nt(high, zwl[t])
        for k in range(4):
            at = pl.multiple_of((t + k) * 16, 16)
            pm[pl.ds(at, 16), :] += total[16 * k : 16 * k + 16, :128]
            pe[pl.ds(at, 16), 0:32] += total[16 * k : 16 * k + 16, 128:160]
        return carry

    lax.fori_loop(0, TILES, spread, 0)

    lane16 = lax.broadcasted_iota(jnp.int32, (16, 128), 1)
    index16 = lane16 & 15
    zero16 = jnp.zeros((16, 128), f32)
    zr = [zero16, zero16]
    zl = [zero16, zero16]
    for n in range(CX + 3):
        x = n - 1
        part, slot = (0, x) if 0 <= x < 8 else (1, x % 8)
        e = pe[pl.ds(16 * n, 16), :]
        er = jnp.where(lane16 < 16, e, 0.0)
        el = jnp.where((lane16 >= 16) & (lane16 < 32), e, 0.0)
        zr[part] = zr[part] + pltpu.roll(er, 16 * slot, 1)
        zl[part] = zl[part] + pltpu.roll(el, (16 * slot + 112) % 128, 1)
    ends = []
    for part in range(2):
        ends.append(
            jnp.where(
                (index16 == 1) | (index16 == 2),
                pltpu.roll(zr[part], 120, 1),
                jnp.where(index16 == 8, pltpu.roll(zl[part], 8, 1), 0.0),
            )
        )
        for half in range(2):
            zbuf[0, half, part] = zr[part][8 * half : 8 * half + 8]
            zbuf[1, half, part] = zl[part][8 * half : 8 * half + 8]
    flat = [m for m in FOLD if m[2] == 0]
    for n, (dx, dy, _) in enumerate(flat):
        half, part = int(dy != 0), int(dx != 0)
        sbuf[n, 0:8] = ends[part][8 * half : 8 * half + 8]
        if dx == 0:
            rows = (15,) if dy < 0 else (8, 9)
            for m, r in enumerate(rows):
                sbuf[n, 8 + 8 * m : 16 + 8 * m] = pm[pl.ds(16 + r, 8, stride=16), :]
        else:
            planes = (0,) if dx < 0 else (9, 10)
            for m, r in enumerate(planes):
                sbuf[n, 8 + 8 * m : 16 + 8 * m] = pm[pl.ds(16 * r + 8 * half, 8), :]

    pl.semaphore_wait(barrier, len(PEERS))

    fold = []
    for n, (dx, dy, dz) in enumerate(FOLD):
        if dz:
            side = 0 if dz > 0 else 1
            src = zbuf.at[side, int(dy != 0), int(dx != 0)]
            dst = rz.at[n]
        else:
            m = flat.index((dx, dy, dz))
            rows = 16 if (dx < 0 or (dx == 0 and dy < 0)) else 24
            src = sbuf.at[m, pl.ds(0, rows)]
            dst = r0.at[m, pl.ds(0, rows)]
        copy = pltpu.make_async_remote_copy(
            src_ref=src, dst_ref=dst, send_sem=send1.at[n], recv_sem=recv1.at[n],
            device_id=device_at(dx, dy, dz), device_id_type=MESH,
        )
        copy.start()
        fold.append(copy)

    def slopes(t, carry):
        zpos = z_position(t)
        for c in range(ZROWS // 16):
            zz = zrow[pl.ds(16 * c, 16), :]
            u = jnp.concatenate([zz] * 4, axis=1) - zpos
            high, low = split(bslope(u))
            zsh[t, pl.ds(16 * c, 16), :] = high
            zsl[t, pl.ds(16 * c, 16), :] = low
        return carry

    lax.fori_loop(0, TILES, slopes, 0)

    for copy in fold:
        copy.wait_recv()

    row8 = lax.broadcasted_iota(jnp.int32, (8, 128), 0)
    lane8 = lax.broadcasted_iota(jnp.int32, (8, 128), 1)
    slot8 = lane8 // 16
    index8 = lane8 & 15

    def rows_of(dy, value):
        if dy == 0:
            return value
        return jnp.where((row8 < 2) if dy > 0 else (row8 == 7), value, 0.0)

    def slots_of(dx, value):
        if dx == 0:
            return value
        return jnp.where((slot8 < 2) if dx > 0 else (slot8 == 7), value, 0.0)

    low_end = jnp.zeros((8, 128), f32)
    high_end = jnp.zeros((8, 128), f32)
    own_end = ends[0][0:8]
    plane = [pm[pl.ds(16 * (x + 1), 8), :] for x in range(CX)]
    for n, (dx, dy, dz) in enumerate(FOLD):
        if dz > 0:
            low_end = low_end + slots_of(dx, rows_of(dy, rz[n]))
        elif dz < 0:
            high_end = high_end + slots_of(dx, rows_of(dy, rz[n]))
        else:
            m = flat.index((dx, dy, dz))
            own_end = own_end + slots_of(dx, rows_of(dy, r0[m, 0:8]))
            if dx > 0:
                plane[0] = plane[0] + rows_of(dy, r0[m, 8:16])
                plane[1] = plane[1] + rows_of(dy, r0[m, 16:24])
            elif dx < 0:
                plane[7] = plane[7] + rows_of(dy, r0[m, 8:16])
    for x in range(CX):
        down = pltpu.roll(low_end, (-(16 * x + 9)) % 128, 1)
        up = pltpu.roll(high_end, (127 - 16 * x) % 128, 1)
        add = jnp.where(lane8 < 2, down, jnp.where(lane8 == 127, up, 0.0))
        fm[pl.ds(8 * x, 8), :] = plane[x] + add
    after, before = flat.index((0, 1, 0)), flat.index((0, -1, 0))
    fm[pl.ds(7, 8, stride=8), :] += r0[before, 8:16]
    fm[pl.ds(0, 8, stride=8), :] += r0[after, 8:16]
    fm[pl.ds(1, 8, stride=8), :] += r0[after, 16:24]
    left = jnp.where(
        index8 < 8, low_end, jnp.where(index8 == 8, low_end + own_end, 0.0)
    )
    right = jnp.where((index8 == 1) | (index8 == 2), high_end + own_end, high_end)
    both_ends = jnp.concatenate([left, right], axis=0).astype(bf16)
    hb[0:16] = both_ends
    hb[80:96] = both_ends
    for m in range(4):
        hb[16 + 16 * m : 32 + 16 * m] = fm[pl.ds(16 * m, 16), :].astype(bf16)

    halo = []
    for n, (dx, dy) in enumerate(HALO):
        start, rows = {2: (64, 32), -2: (0, 32)}.get(dx, (0, 80))
        copy = pltpu.make_async_remote_copy(
            src_ref=hb.at[pl.ds(start, rows)], dst_ref=rh.at[n, pl.ds(0, rows)],
            send_sem=send2.at[n], recv_sem=recv2.at[n],
            device_id=device_at(dx, dy, 0), device_id_type=MESH,
        )
        copy.start()
        halo.append(copy)

    xf[...] = jnp.zeros_like(xf)
    for i in range(SPAN):
        xf[32 * (i + 1) : 32 * (i + 1) + SPAN, 0:SPAN] = kern_ref[i].astype(f32)
    xb = xf[...].astype(bf16)
    eye = (
        lax.broadcasted_iota(jnp.int32, (24, 128), 0)
        == lax.broadcasted_iota(jnp.int32, (24, 128), 1)
    ).astype(f32).astype(bf16)
    blocks = []
    for h in range(2):
        kt = mm_nt(eye, xb[32 * (1 - h) : 32 * (1 - h) + 640])
        blocks += [kt[:, 128 * g : 128 * g + 128] for g in range(5)]
    lhs = jnp.concatenate(blocks, axis=0).astype(bf16)
    drow = lax.broadcasted_iota(jnp.int32, (128, 128), 0)
    dlane = lax.broadcasted_iota(jnp.int32, (128, 128), 1)
    base = (drow >> 6) * 64 + ((drow >> 5) & 1) * 8

    def shifted(n, carry):
        r = jnp.where(n < 10, n, 15)
        y = jnp.where(n < 10, n, -1)
        jy = ((drow & 31) + y) & 31
        target = base + (jy >> 3) * 16 + (jy & 7)
        sel = (dlane == target).astype(f32).astype(bf16)
        out = mm(lhs, sel)
        for h in range(2):
            for g in range(5):
                for c in range(3):
                    at = h * 120 + g * 24 + 8 * c
                    tf[g, pl.ds(h * 384 + 128 * c + r, 8, stride=16), :] = out[at : at + 8]
        return carry

    lax.fori_loop(0, 11, shifted, 0)
    for h in range(2):
        for g in range(5):
            for r in range(10, 15):
                for c in range(3):
                    tf[g, pl.ds(h * 384 + 128 * c + r, 8, stride=16), :] = jnp.zeros((8, 128), f32)
            tb[272 * h : 272 * h + 272, 128 * g : 128 * g + 128] = (
                tf[g, 384 * h : 384 * h + 272, :].astype(bf16)
            )

    def place(ends_bf16, main, xp, b, slots):
        at = xp * 64 + b * 16
        w[at : at + 16, 0:128] = main
        wide = ends_bf16.astype(f32)
        tops = []
        for s in slots:
            lo = pltpu.roll(wide[0:8], (119 - 16 * s) % 128, 1)
            hi = pltpu.roll(wide[8:16], (-1 - 16 * s) % 128, 1)
            tops.append(jnp.where(lane8 < 64, hi, lo))
        w[at : at + 16, 128:256] = jnp.concatenate(tops, axis=0).astype(bf16)

    for m in range(4):
        place(hb[0:16], hb[16 + 16 * m : 32 + 16 * m], 5 + m, 1, (2 * m, 2 * m + 1))
    for n, copy in enumerate(halo):
        copy.wait_recv()
    for n, (dx, dy) in enumerate(HALO):
        sx, b = -dx, (1 - dy) % 4
        if sx == 2:
            place(rh[n, 0:16], rh[n, 16:32], 13, b, (0, 1))
        elif sx == -2:
            place(rh[n, 16:32], rh[n, 0:16], 0, b, (6, 7))
        else:
            for m in range(4):
                place(
                    rh[n, 0:16], rh[n, 16 + 16 * m : 32 + 16 * m],
                    4 * sx + 5 + m, b, (2 * m, 2 * m + 1),
                )

    def convolve(p, carry):
        rhs = w[pl.ds(pl.multiple_of(64 * p, 64), 576), :]
        out = mm(tb[:, 0:576], rhs)
        for h in range(2):
            acc = None
            for k in range(SPAN):
                term = out[272 * h + 16 * k : 272 * h + 16 * k + 16]
                if k != 8:
                    term = pltpu.roll(term, (8 - k) % 256, 1)
                acc = term if acc is None else acc + term
            main, far = acc[:, 0:128], acc[:, 128:256]
            tail = jnp.where(
                (lane16 == 9) | (lane16 == 10),
                pltpu.roll(far, 9, 1),
                jnp.where(lane16 == 16, pltpu.roll(far, 17, 1), 0.0),
            )
            at = pl.multiple_of((2 * p + h) * 16, 16)
            mh, ml = split(main)
            th, tl = split(tail)
            phh[pl.ds(at, 16), 0:128] = mh
            phh[pl.ds(at, 16), 128:256] = th
            phl[pl.ds(at, 16), 0:128] = ml
            phl[pl.ds(at, 16), 128:256] = tl

            @pl.when((p >= 1) & (p <= 4))
            def _():
                pot_ref[2 * p + h - 2] = main[0:8]

        return carry

    lax.fori_loop(0, 6, convolve, 0)

    def interpolate(t, carry):
        at = pl.multiple_of((t + 1) * 16, 16)
        high = phh[pl.ds(at, 64), 0:ZROWS]
        both = jnp.concatenate([high, phl[pl.ds(at, 64), 0:ZROWS]], axis=0)
        a = mm(both, zwh[t])
        value = a[:64] + a[64:] + mm(high, zwl[t])
        a = mm(both, zsh[t])
        slope = a[:64] + a[64:] + mm(high, zsl[t])
        u = y_distance(t)
        wy, sy = bspline(u), bslope(u)
        wx, sx = x_splines(off_ref[0, t, 0])
        fx = fy = fz = None
        for k in range(4):
            v, s = value[16 * k : 16 * k + 16], slope[16 * k : 16 * k + 16]
            ax, ay, az = sx[k] * v, wx[k] * v, wx[k] * s
            fx = ax if fx is None else fx + ax
            fy = ay if fy is None else fy + ay
            fz = az if fz is None else fz + az
        charge = -q_ref[t, 0]
        frc_ref[0, t, 0] = charge * jnp.sum(fx * wy, axis=0, keepdims=True)
        frc_ref[1, t, 0] = charge * jnp.sum(fy * sy, axis=0, keepdims=True)
        frc_ref[2, t, 0] = charge * jnp.sum(fz * wy, axis=0, keepdims=True)
        return carry

    lax.fori_loop(0, TILES, interpolate, 0)

    for copy in fold:
        copy.wait_send()
    for copy in halo:
        copy.wait_send()


def local(charges, offsets, cells, kernel):
    f32, bf16 = jnp.float32, jnp.bfloat16
    vmem = pl.BlockSpec(memory_space=pltpu.VMEM)
    return pl.pallas_call(
        body,
        out_shape=(
            jax.ShapeDtypeStruct((CX, CY, CZ), f32),
            jax.ShapeDtypeStruct((3, TILES, 1, 1, APT), f32),
        ),
        in_specs=[vmem] * 4,
        out_specs=(vmem, vmem),
        scratch_shapes=[
            pltpu.VMEM((ZROWS, 128), f32),
            pltpu.VMEM((TILES, ZROWS, APT), bf16),
            pltpu.VMEM((TILES, ZROWS, APT), bf16),
            pltpu.VMEM((TILES, ZROWS, APT), bf16),
            pltpu.VMEM((TILES, ZROWS, APT), bf16),
            pltpu.VMEM((16 * (CX + 3), 128), f32),
            pltpu.VMEM((16 * (CX + 3), 128), f32),
            pltpu.VMEM((2, 2, 2, 8, 128), f32),
            pltpu.VMEM((8, 24, 128), f32),
            pltpu.VMEM((18, 8, 128), f32),
            pltpu.VMEM((8, 24, 128), f32),
            pltpu.VMEM((64, 128), f32),
            pltpu.VMEM((96, 128), bf16),
            pltpu.VMEM((len(HALO), 80, 128), bf16),
            pltpu.VMEM((32 * 21, 128), f32),
            pltpu.VMEM((5, 768, 128), f32),
            pltpu.VMEM((544, 640), bf16),
            pltpu.VMEM((14 * 64, 256), bf16),
            pltpu.VMEM((192, 256), bf16),
            pltpu.VMEM((192, 256), bf16),
            pltpu.SemaphoreType.DMA((len(FOLD),)),
            pltpu.SemaphoreType.DMA((len(FOLD),)),
            pltpu.SemaphoreType.DMA((len(HALO),)),
            pltpu.SemaphoreType.DMA((len(HALO),)),
        ],
        compiler_params=pltpu.CompilerParams(
            collective_id=0, has_side_effects=True, vmem_limit_bytes=48 * 1024 * 1024
        ),
    )(charges, offsets, cells, kernel)


def solution(mesh):
    placed = (
        P("gx", "gy", "gz", None),
        P(None, "gx", "gy", "gz", None),
        P(None, "gx", "gy", "gz", None),
        P(),
    )
    return jax.shard_map(
        local,
        mesh=mesh,
        in_specs=placed,
        out_specs=(P("gx", "gy", "gz"), P(None, "gx", "gy", "gz", None)),
        check_vma=False,
    )
```

```python
import jax
import jax.numpy as jnp
from jax import lax
from jax.experimental import pallas as pl
from jax.experimental.pallas import tpu as pltpu
from jax.sharding import PartitionSpec as P

CX = 8
CY = 8
CZ = 128
TILES = 8
APT = 512
SPAN = 17
ZROWS = 160
MESH = pl.DeviceIdType.MESH

FOLD = [
    (dx, dy, dz)
    for dz in (1, -1, 0)
    for dx in (1, -1, 0)
    for dy in (1, -1, 0)
    if (dx, dy, dz) != (0, 0, 0)
]
HALO = [(dx, dy) for dx in (1, -1) for dy in (2, 1, -1, 0)]
HALO += [(dx, dy) for dx in (2, -2) for dy in (2, 1, -1, 0)]
HALO += [(0, dy) for dy in (2, 1, -1)]
PEERS = FOLD


def neighbours():
    tables = []
    for axis in ("gx", "gy", "gz"):
        size = lax.axis_size(axis)
        index = lax.axis_index(axis)
        table = {0: index}
        for step in (1, 2):
            up, down = index + step, index - step
            table[step] = jnp.where(up >= size, up - size, up)
            table[-step] = jnp.where(down < 0, down + size, down)
        table[3] = table[-1]
        tables.append(table)
    return lambda dx, dy, dz: (tables[0][dx], tables[1][dy], tables[2][dz])


def x_splines(f):
    r = 1.0 - f
    values = [
        r * r * r / 6.0,
        (3.0 * f * f * f - 6.0 * f * f + 4.0) / 6.0,
        (-3.0 * f * f * f + 3.0 * f * f + 3.0 * f + 1.0) / 6.0,
        f * f * f / 6.0,
    ]
    slopes = [-0.5 * r * r, 1.5 * f * f - 2.0 * f, -1.5 * f * f + f + 0.5, 0.5 * f * f]
    return values, slopes


def bspline(u):
    a = jnp.abs(u)
    p = jnp.maximum(2.0 - a, 0.0)
    q = jnp.maximum(1.0 - a, 0.0)
    return p * p * p * (1.0 / 6.0) - q * q * q * (2.0 / 3.0)


def bslope(u):
    a = jnp.abs(u)
    p = jnp.maximum(2.0 - a, 0.0)
    q = jnp.maximum(1.0 - a, 0.0)
    m = 0.5 * p * p - 2.0 * q * q
    return jnp.where(u < 0.0, -m, m)


def split(value):
    high = value.astype(jnp.bfloat16)
    low = (value - high.astype(jnp.float32)).astype(jnp.bfloat16)
    return high, low


def mm(a, b):
    return jnp.dot(a, b, preferred_element_type=jnp.float32)


def mm_nt(a, b):
    return lax.dot_general(a, b, (((1,), (1,)), ((), ())), preferred_element_type=jnp.float32)


def body(
    q_hbm, off_hbm, cell_hbm, kern_hbm, pot_ref, frc_ref,
    q_ref, off_ref, cell_ref, kern_ref, ys, xs,
    zrow, zwh, zwl, zsh, zsl, pm, pe, zbuf, sbuf, rz, r0, fm, hb, rh,
    xf, tf, tb, w, phh, phl, load, send1, recv1, send2, recv2,
):
    iy = lax.axis_index("gy")
    iz = lax.axis_index("gz")
    f32, bf16 = jnp.float32, jnp.bfloat16

    device_at = neighbours()
    barrier = pltpu.get_barrier_semaphore()
    for peer in PEERS:
        pl.semaphore_signal(barrier, inc=1, device_id=device_at(*peer), device_id_type=MESH)

    loads = [
        pltpu.make_async_copy(q_hbm.at[:, 0, 0, :], q_ref, load.at[0]),
        pltpu.make_async_copy(off_hbm.at[:, :, 0, 0, :], off_ref, load.at[1]),
        pltpu.make_async_copy(cell_hbm.at[:, :, 0, 0, :], cell_ref, load.at[2]),
        pltpu.make_async_copy(kern_hbm, kern_ref, load.at[3]),
    ]
    for copy in loads:
        copy.start()

    row_id = lax.broadcasted_iota(jnp.int32, (ZROWS, 128), 0)
    zrow[...] = jnp.where(
        row_id < 128, row_id, jnp.where(row_id < 144, row_id - 9, row_id - 145)
    ).astype(f32)
    pm[...] = jnp.zeros_like(pm)
    pe[...] = jnp.zeros_like(pe)
    y_id = lax.broadcasted_iota(jnp.int32, (16, APT), 0)
    y_id = jnp.where(y_id < 15, y_id, -1).astype(f32)

    def y_distance(t):
        ly = (cell_ref[0, pl.ds(t, 1), :] - iy * CY).astype(f32)
        return (y_id - ly) - off_ref[1, pl.ds(t, 1), :]

    def z_position(t):
        return (cell_ref[1, pl.ds(t, 1), :] - iz * CZ).astype(f32) + off_ref[2, pl.ds(t, 1), :]

    for copy in loads:
        copy.wait()
    values, derivatives = x_splines(off_ref[0])
    for k in range(4):
        xs[k] = q_ref[...] * values[k]
        xs[4 + k] = -q_ref[...] * derivatives[k]

    def spread(t, carry):
        zpos = z_position(t)
        for c in range(ZROWS // 16):
            zz = zrow[pl.ds(16 * c, 16), :]
            u = jnp.concatenate([zz] * 4, axis=1) - zpos
            high, low = split(bspline(u))
            zwh[t, pl.ds(16 * c, 16), :] = high
            zwl[t, pl.ds(16 * c, 16), :] = low
        wy = bspline(y_distance(t))
        ys[0, t] = wy
        parts = [split(xs[k, pl.ds(t, 1), :] * wy) for k in range(4)]
        high = jnp.concatenate([p[0] for p in parts], axis=0)
        both = jnp.concatenate([high] + [p[1] for p in parts], axis=0)
        first = mm_nt(both, zwh[t])
        total = first[:64] + first[64:] + mm_nt(high, zwl[t])
        for k in range(4):
            at = pl.multiple_of((t + k) * 16, 16)
            pm[pl.ds(at, 16), :] += total[16 * k : 16 * k + 16, :128]
            pe[pl.ds(at, 16), 0:32] += total[16 * k : 16 * k + 16, 128:160]
        return carry

    lax.fori_loop(0, TILES, spread, 0, unroll=2)

    lane16 = lax.broadcasted_iota(jnp.int32, (16, 128), 1)
    index16 = lane16 & 15
    zero16 = jnp.zeros((16, 128), f32)
    zr = [zero16, zero16]
    zl = [zero16, zero16]
    for n in range(CX + 3):
        x = n - 1
        part, slot = (0, x) if 0 <= x < 8 else (1, x % 8)
        e = pe[pl.ds(16 * n, 16), :]
        er = jnp.where(lane16 < 16, e, 0.0)
        el = jnp.where((lane16 >= 16) & (lane16 < 32), e, 0.0)
        zr[part] = zr[part] + pltpu.roll(er, 16 * slot, 1)
        zl[part] = zl[part] + pltpu.roll(el, (16 * slot + 112) % 128, 1)
    ends = []
    for part in range(2):
        ends.append(
            jnp.where(
                (index16 == 1) | (index16 == 2),
                pltpu.roll(zr[part], 120, 1),
                jnp.where(index16 == 8, pltpu.roll(zl[part], 8, 1), 0.0),
            )
        )
        for half in range(2):
            zbuf[0, half, part] = zr[part][8 * half : 8 * half + 8]
            zbuf[1, half, part] = zl[part][8 * half : 8 * half + 8]
    flat = [m for m in FOLD if m[2] == 0]
    for n, (dx, dy, _) in enumerate(flat):
        half, part = int(dy != 0), int(dx != 0)
        sbuf[n, 0:8] = ends[part][8 * half : 8 * half + 8]
        if dx == 0:
            rows = (15,) if dy < 0 else (8, 9)
            for m, r in enumerate(rows):
                sbuf[n, 8 + 8 * m : 16 + 8 * m] = pm[pl.ds(16 + r, 8, stride=16), :]
        else:
            planes = (0,) if dx < 0 else (9, 10)
            for m, r in enumerate(planes):
                sbuf[n, 8 + 8 * m : 16 + 8 * m] = pm[pl.ds(16 * r + 8 * half, 8), :]

    pl.semaphore_wait(barrier, len(PEERS))

    fold = []
    for n, (dx, dy, dz) in enumerate(FOLD):
        if dz:
            side = 0 if dz > 0 else 1
            src = zbuf.at[side, int(dy != 0), int(dx != 0)]
            dst = rz.at[n]
        else:
            m = flat.index((dx, dy, dz))
            rows = 16 if (dx < 0 or (dx == 0 and dy < 0)) else 24
            src = sbuf.at[m, pl.ds(0, rows)]
            dst = r0.at[m, pl.ds(0, rows)]
        copy = pltpu.make_async_remote_copy(
            src_ref=src, dst_ref=dst, send_sem=send1.at[n], recv_sem=recv1.at[n],
            device_id=device_at(dx, dy, dz), device_id_type=MESH,
        )
        copy.start()
        fold.append(copy)

    def slopes(t, carry):
        zpos = z_position(t)
        ys[1, t] = bslope(y_distance(t))
        for c in range(ZROWS // 16):
            zz = zrow[pl.ds(16 * c, 16), :]
            u = jnp.concatenate([zz] * 4, axis=1) - zpos
            high, low = split(bslope(u))
            zsh[t, pl.ds(16 * c, 16), :] = high
            zsl[t, pl.ds(16 * c, 16), :] = low
        return carry

    lax.fori_loop(0, TILES, slopes, 0)

    for copy in fold:
        copy.wait_recv()

    row8 = lax.broadcasted_iota(jnp.int32, (8, 128), 0)
    lane8 = lax.broadcasted_iota(jnp.int32, (8, 128), 1)
    slot8 = lane8 // 16
    index8 = lane8 & 15

    def rows_of(dy, value):
        if dy == 0:
            return value
        return jnp.where((row8 < 2) if dy > 0 else (row8 == 7), value, 0.0)

    def slots_of(dx, value):
        if dx == 0:
            return value
        return jnp.where((slot8 < 2) if dx > 0 else (slot8 == 7), value, 0.0)

    low_end = jnp.zeros((8, 128), f32)
    high_end = jnp.zeros((8, 128), f32)
    own_end = ends[0][0:8]
    plane = [pm[pl.ds(16 * (x + 1), 8), :] for x in range(CX)]
    for n, (dx, dy, dz) in enumerate(FOLD):
        if dz > 0:
            low_end = low_end + slots_of(dx, rows_of(dy, rz[n]))
        elif dz < 0:
            high_end = high_end + slots_of(dx, rows_of(dy, rz[n]))
        else:
            m = flat.index((dx, dy, dz))
            own_end = own_end + slots_of(dx, rows_of(dy, r0[m, 0:8]))
            if dx > 0:
                plane[0] = plane[0] + rows_of(dy, r0[m, 8:16])
                plane[1] = plane[1] + rows_of(dy, r0[m, 16:24])
            elif dx < 0:
                plane[7] = plane[7] + rows_of(dy, r0[m, 8:16])
    for x in range(CX):
        down = pltpu.roll(low_end, (-(16 * x + 9)) % 128, 1)
        up = pltpu.roll(high_end, (127 - 16 * x) % 128, 1)
        add = jnp.where(lane8 < 2, down, jnp.where(lane8 == 127, up, 0.0))
        fm[pl.ds(8 * x, 8), :] = plane[x] + add
    after, before = flat.index((0, 1, 0)), flat.index((0, -1, 0))
    fm[pl.ds(7, 8, stride=8), :] += r0[before, 8:16]
    fm[pl.ds(0, 8, stride=8), :] += r0[after, 8:16]
    fm[pl.ds(1, 8, stride=8), :] += r0[after, 16:24]
    left = jnp.where(
        index8 < 8, low_end, jnp.where(index8 == 8, low_end + own_end, 0.0)
    )
    right = jnp.where((index8 == 1) | (index8 == 2), high_end + own_end, high_end)
    both_ends = jnp.concatenate([left, right], axis=0).astype(bf16)
    hb[0:16] = both_ends
    hb[80:96] = both_ends
    for m in range(4):
        hb[16 + 16 * m : 32 + 16 * m] = fm[pl.ds(16 * m, 16), :].astype(bf16)

    halo = []
    for n, (dx, dy) in enumerate(HALO):
        start, rows = {2: (64, 32), -2: (0, 32)}.get(dx, (0, 80))
        copy = pltpu.make_async_remote_copy(
            src_ref=hb.at[pl.ds(start, rows)], dst_ref=rh.at[n, pl.ds(0, rows)],
            send_sem=send2.at[n], recv_sem=recv2.at[n],
            device_id=device_at(dx, dy, 0), device_id_type=MESH,
        )
        copy.start()
        halo.append(copy)

    xf[...] = jnp.zeros_like(xf)
    for i in range(SPAN):
        xf[32 * (i + 1) : 32 * (i + 1) + SPAN, 0:SPAN] = kern_ref[i].astype(f32)
    xb = xf[...].astype(bf16)
    eye = (
        lax.broadcasted_iota(jnp.int32, (24, 128), 0)
        == lax.broadcasted_iota(jnp.int32, (24, 128), 1)
    ).astype(f32).astype(bf16)
    blocks = []
    for h in range(2):
        kt = mm_nt(eye, xb[32 * (1 - h) : 32 * (1 - h) + 640])
        blocks += [kt[:, 128 * g : 128 * g + 128] for g in range(5)]
    lhs = jnp.concatenate(blocks, axis=0).astype(bf16)
    drow = lax.broadcasted_iota(jnp.int32, (128, 128), 0)
    dlane = lax.broadcasted_iota(jnp.int32, (128, 128), 1)
    base = (drow >> 6) * 64 + ((drow >> 5) & 1) * 8

    def shifted(n, carry):
        r = jnp.where(n < 10, n, 15)
        y = jnp.where(n < 10, n, -1)
        jy = ((drow & 31) + y) & 31
        target = base + (jy >> 3) * 16 + (jy & 7)
        sel = (dlane == target).astype(f32).astype(bf16)
        out = mm(lhs, sel)
        for h in range(2):
            for g in range(5):
                for c in range(3):
                    at = h * 120 + g * 24 + 8 * c
                    tf[g, pl.ds(h * 384 + 128 * c + r, 8, stride=16), :] = out[at : at + 8]
        return carry

    lax.fori_loop(0, 11, shifted, 0)
    for h in range(2):
        for g in range(5):
            for r in range(10, 15):
                for c in range(3):
                    tf[g, pl.ds(h * 384 + 128 * c + r, 8, stride=16), :] = jnp.zeros((8, 128), f32)
            tb[272 * h : 272 * h + 272, 128 * g : 128 * g + 128] = (
                tf[g, 384 * h : 384 * h + 272, :].astype(bf16)
            )

    def place(ends_bf16, main, xp, b, slots):
        at = xp * 64 + b * 16
        w[at : at + 16, 0:128] = main
        wide = ends_bf16.astype(f32)
        tops = []
        for s in slots:
            lo = pltpu.roll(wide[0:8], (119 - 16 * s) % 128, 1)
            hi = pltpu.roll(wide[8:16], (-1 - 16 * s) % 128, 1)
            tops.append(jnp.where(lane8 < 64, hi, lo))
        w[at : at + 16, 128:256] = jnp.concatenate(tops, axis=0).astype(bf16)

    for m in range(4):
        place(hb[0:16], hb[16 + 16 * m : 32 + 16 * m], 5 + m, 1, (2 * m, 2 * m + 1))
    for n, copy in enumerate(halo):
        copy.wait_recv()
    for n, (dx, dy) in enumerate(HALO):
        sx, b = -dx, (1 - dy) % 4
        if sx == 2:
            place(rh[n, 0:16], rh[n, 16:32], 13, b, (0, 1))
        elif sx == -2:
            place(rh[n, 16:32], rh[n, 0:16], 0, b, (6, 7))
        else:
            for m in range(4):
                place(
                    rh[n, 0:16], rh[n, 16 + 16 * m : 32 + 16 * m],
                    4 * sx + 5 + m, b, (2 * m, 2 * m + 1),
                )

    for p in range(6):
        skip = 272 if p == 0 else 0
        out = mm(tb[skip:544, 0:576], w[64 * p : 64 * p + 576, :])
        for h in range(skip // 272, 2):
            acc = None
            for k in range(SPAN):
                at = 272 * h + 16 * k - skip
                term = out[at : at + 16]
                if k != 8:
                    term = pltpu.roll(term, (8 - k) % 256, 1)
                acc = term if acc is None else acc + term
            main, far = acc[:, 0:128], acc[:, 128:256]
            tail = jnp.where(
                (lane16 == 9) | (lane16 == 10),
                pltpu.roll(far, 9, 1),
                jnp.where(lane16 == 16, pltpu.roll(far, 17, 1), 0.0),
            )
            at = (2 * p + h) * 16
            mh, ml = split(main)
            th, tl = split(tail)
            phh[at : at + 16, 0:128] = mh
            phh[at : at + 16, 128:256] = th
            phl[at : at + 16, 0:128] = ml
            phl[at : at + 16, 128:256] = tl
            if 1 <= p <= 4:
                pot_ref[2 * p + h - 2] = main[0:8]

    for t in range(TILES):
        at = (t + 1) * 16
        high = phh[at : at + 64, 0:ZROWS]
        both = jnp.concatenate([high, phl[at : at + 64, 0:ZROWS]], axis=0)
        a = mm(both, zwh[t])
        value = a[:64] + a[64:] + mm(high, zwl[t])
        a = mm(both, zsh[t])
        slope = a[:64] + a[64:] + mm(high, zsl[t])
        fx = fy = fz = None
        for k in range(4):
            v, s = value[16 * k : 16 * k + 16], slope[16 * k : 16 * k + 16]
            wx, sx = xs[k, t : t + 1, :], xs[4 + k, t : t + 1, :]
            ax, ay, az = sx * v, wx * v, wx * s
            fx = ax if fx is None else fx + ax
            fy = ay if fy is None else fy + ay
            fz = az if fz is None else fz + az
        wy, sy = ys[0, t], ys[1, t]
        frc_ref[0, t, 0] = jnp.sum(fx * wy, axis=0, keepdims=True)
        frc_ref[1, t, 0] = -jnp.sum(fy * sy, axis=0, keepdims=True)
        frc_ref[2, t, 0] = -jnp.sum(fz * wy, axis=0, keepdims=True)

    for copy in fold:
        copy.wait_send()
    for copy in halo:
        copy.wait_send()


def local(charges, offsets, cells, kernel):
    f32, bf16 = jnp.float32, jnp.bfloat16
    vmem = pl.BlockSpec(memory_space=pltpu.VMEM)
    return pl.pallas_call(
        body,
        out_shape=(
            jax.ShapeDtypeStruct((CX, CY, CZ), f32),
            jax.ShapeDtypeStruct((3, TILES, 1, 1, APT), f32),
        ),
        in_specs=[pl.BlockSpec(memory_space=pltpu.HBM)] * 4,
        out_specs=(vmem, vmem),
        scratch_shapes=[
            pltpu.VMEM((TILES, APT), f32),
            pltpu.VMEM((3, TILES, APT), f32),
            pltpu.VMEM((2, TILES, APT), jnp.int32),
            pltpu.VMEM((SPAN, SPAN, SPAN), bf16),
            pltpu.VMEM((2, TILES, 16, APT), f32),
            pltpu.VMEM((8, TILES, APT), f32),
            pltpu.VMEM((ZROWS, 128), f32),
            pltpu.VMEM((TILES, ZROWS, APT), bf16),
            pltpu.VMEM((TILES, ZROWS, APT), bf16),
            pltpu.VMEM((TILES, ZROWS, APT), bf16),
            pltpu.VMEM((TILES, ZROWS, APT), bf16),
            pltpu.VMEM((16 * (CX + 3), 128), f32),
            pltpu.VMEM((16 * (CX + 3), 128), f32),
            pltpu.VMEM((2, 2, 2, 8, 128), f32),
            pltpu.VMEM((8, 24, 128), f32),
            pltpu.VMEM((18, 8, 128), f32),
            pltpu.VMEM((8, 24, 128), f32),
            pltpu.VMEM((64, 128), f32),
            pltpu.VMEM((96, 128), bf16),
            pltpu.VMEM((len(HALO), 80, 128), bf16),
            pltpu.VMEM((32 * 21, 128), f32),
            pltpu.VMEM((5, 768, 128), f32),
            pltpu.VMEM((544, 640), bf16),
            pltpu.VMEM((14 * 64, 256), bf16),
            pltpu.VMEM((192, 256), bf16),
            pltpu.VMEM((192, 256), bf16),
            pltpu.SemaphoreType.DMA((4,)),
            pltpu.SemaphoreType.DMA((len(FOLD),)),
            pltpu.SemaphoreType.DMA((len(FOLD),)),
            pltpu.SemaphoreType.DMA((len(HALO),)),
            pltpu.SemaphoreType.DMA((len(HALO),)),
        ],
        compiler_params=pltpu.CompilerParams(
            collective_id=0, has_side_effects=True, vmem_limit_bytes=64 * 1024 * 1024
        ),
    )(charges, offsets, cells, kernel)


def solution(mesh):
    placed = (
        P("gx", "gy", "gz", None),
        P(None, "gx", "gy", "gz", None),
        P(None, "gx", "gy", "gz", None),
        P(),
    )
    return jax.shard_map(
        local,
        mesh=mesh,
        in_specs=placed,
        out_specs=(P("gx", "gy", "gz"), P(None, "gx", "gy", "gz", None)),
        check_vma=False,
    )
```

```python
import jax
import jax.numpy as jnp
from jax import lax
from jax.experimental import pallas as pl
from jax.experimental.pallas import tpu as pltpu
from jax.sharding import PartitionSpec as P

CX = 8
CY = 8
CZ = 128
TILES = 8
APT = 512
SPAN = 17
ZROWS = 160
MESH = pl.DeviceIdType.MESH

FOLD = [
    (dx, dy, dz)
    for dx in (1, 0, -1)
    for dy, dz in ((1, 1), (-1, 1), (1, -1), (-1, -1), (0, 1), (0, -1), (1, 0), (-1, 0), (0, 0))
    if (dx, dy, dz) != (0, 0, 0)
]
HALO = [(dx, dy) for dy in (2, 1, -1, 0) for dx in (2, 1)]
HALO += [(0, dy) for dy in (2, 1, -1)]
HALO += [(dx, dy) for dy in (2, 1, -1, 0) for dx in (-2, -1)]
PEERS = FOLD


def neighbours():
    tables = []
    for axis in ("gx", "gy", "gz"):
        size = lax.axis_size(axis)
        index = lax.axis_index(axis)
        table = {0: index}
        for step in (1, 2):
            up, down = index + step, index - step
            table[step] = jnp.where(up >= size, up - size, up)
            table[-step] = jnp.where(down < 0, down + size, down)
        table[3] = table[-1]
        tables.append(table)
    return lambda dx, dy, dz: (tables[0][dx], tables[1][dy], tables[2][dz])


def x_splines(f):
    r = 1.0 - f
    values = [
        r * r * r / 6.0,
        (3.0 * f * f * f - 6.0 * f * f + 4.0) / 6.0,
        (-3.0 * f * f * f + 3.0 * f * f + 3.0 * f + 1.0) / 6.0,
        f * f * f / 6.0,
    ]
    slopes = [-0.5 * r * r, 1.5 * f * f - 2.0 * f, -1.5 * f * f + f + 0.5, 0.5 * f * f]
    return values, slopes


def bspline(u):
    a = jnp.abs(u)
    p = jnp.maximum(2.0 - a, 0.0)
    q = jnp.maximum(1.0 - a, 0.0)
    return p * p * p * (1.0 / 6.0) - q * q * q * (2.0 / 3.0)


def bslope(u):
    a = jnp.abs(u)
    p = jnp.maximum(2.0 - a, 0.0)
    q = jnp.maximum(1.0 - a, 0.0)
    m = 0.5 * p * p - 2.0 * q * q
    return jnp.where(u < 0.0, -m, m)


def split(value):
    high = value.astype(jnp.bfloat16)
    low = (value - high.astype(jnp.float32)).astype(jnp.bfloat16)
    return high, low


def mm(a, b):
    return jnp.dot(a, b, preferred_element_type=jnp.float32)


def mm_nt(a, b):
    return lax.dot_general(a, b, (((1,), (1,)), ((), ())), preferred_element_type=jnp.float32)


def body(
    q_hbm, off_hbm, cell_hbm, kern_hbm, pot_ref, frc_ref,
    q_ref, off_ref, cell_ref, kern_ref, ys, xs,
    zrow, zwh, zwl, zsh, zsl, pm, pe, zbuf, sbuf, rz, r0, fm, hb, rh,
    xf, tf, tb, w, phh, phl, load, send1, recv1, send2, recv2,
):
    iy = lax.axis_index("gy")
    iz = lax.axis_index("gz")
    f32, bf16 = jnp.float32, jnp.bfloat16

    device_at = neighbours()
    barrier = pltpu.get_barrier_semaphore()
    for peer in PEERS:
        pl.semaphore_signal(barrier, inc=1, device_id=device_at(*peer), device_id_type=MESH)

    loads = [
        pltpu.make_async_copy(q_hbm.at[:, 0, 0, :], q_ref, load.at[0]),
        pltpu.make_async_copy(off_hbm.at[:, :, 0, 0, :], off_ref, load.at[1]),
        pltpu.make_async_copy(cell_hbm.at[:, :, 0, 0, :], cell_ref, load.at[2]),
        pltpu.make_async_copy(kern_hbm, kern_ref, load.at[3]),
    ]
    for copy in loads:
        copy.start()

    row_id = lax.broadcasted_iota(jnp.int32, (ZROWS, 128), 0)
    zrow[...] = jnp.where(
        row_id < 128, row_id, jnp.where(row_id < 144, row_id - 9, row_id - 145)
    ).astype(f32)
    pm[...] = jnp.zeros_like(pm)
    pe[...] = jnp.zeros_like(pe)
    y_id = lax.broadcasted_iota(jnp.int32, (16, APT), 0)
    y_id = jnp.where(y_id < 15, y_id, -1).astype(f32)

    def y_distance(t):
        ly = (cell_ref[0, pl.ds(t, 1), :] - iy * CY).astype(f32)
        return (y_id - ly) - off_ref[1, pl.ds(t, 1), :]

    def z_position(t):
        return (cell_ref[1, pl.ds(t, 1), :] - iz * CZ).astype(f32) + off_ref[2, pl.ds(t, 1), :]

    for copy in loads:
        copy.wait()
    values, derivatives = x_splines(off_ref[0])
    for k in range(4):
        xs[k] = q_ref[...] * values[k]
        xs[4 + k] = -q_ref[...] * derivatives[k]

    def spread(t, carry):
        zpos = z_position(t)
        for c in range(ZROWS // 16):
            zz = zrow[pl.ds(16 * c, 16), :]
            u = jnp.concatenate([zz] * 4, axis=1) - zpos
            high, low = split(bspline(u))
            zwh[t, pl.ds(16 * c, 16), :] = high
            zwl[t, pl.ds(16 * c, 16), :] = low
        wy = bspline(y_distance(t))
        ys[0, t] = wy
        parts = [split(xs[k, pl.ds(t, 1), :] * wy) for k in range(4)]
        high = jnp.concatenate([p[0] for p in parts], axis=0)
        both = jnp.concatenate([high] + [p[1] for p in parts], axis=0)
        first = mm_nt(both, zwh[t])
        total = first[:64] + first[64:] + mm_nt(high, zwl[t])
        for k in range(4):
            at = pl.multiple_of((t + k) * 16, 16)
            pm[pl.ds(at, 16), :] += total[16 * k : 16 * k + 16, :128]
            pe[pl.ds(at, 16), 0:32] += total[16 * k : 16 * k + 16, 128:160]
        return carry

    lax.fori_loop(0, TILES, spread, 0, unroll=2)

    lane16 = lax.broadcasted_iota(jnp.int32, (16, 128), 1)
    index16 = lane16 & 15
    zero16 = jnp.zeros((16, 128), f32)
    zr = [zero16, zero16]
    zl = [zero16, zero16]
    for n in range(CX + 3):
        x = n - 1
        part, slot = (0, x) if 0 <= x < 8 else (1, x % 8)
        e = pe[pl.ds(16 * n, 16), :]
        er = jnp.where(lane16 < 16, e, 0.0)
        el = jnp.where((lane16 >= 16) & (lane16 < 32), e, 0.0)
        zr[part] = zr[part] + pltpu.roll(er, 16 * slot, 1)
        zl[part] = zl[part] + pltpu.roll(el, (16 * slot + 112) % 128, 1)
    ends = []
    for part in range(2):
        ends.append(
            jnp.where(
                (index16 == 1) | (index16 == 2),
                pltpu.roll(zr[part], 120, 1),
                jnp.where(index16 == 8, pltpu.roll(zl[part], 8, 1), 0.0),
            )
        )
        for half in range(2):
            zbuf[0, half, part] = zr[part][8 * half : 8 * half + 8]
            zbuf[1, half, part] = zl[part][8 * half : 8 * half + 8]
    flat = [m for m in FOLD if m[2] == 0]
    for n, (dx, dy, _) in enumerate(flat):
        half, part = int(dy != 0), int(dx != 0)
        sbuf[n, 0:8] = ends[part][8 * half : 8 * half + 8]
        if dx == 0:
            rows = (15,) if dy < 0 else (8, 9)
            for m, r in enumerate(rows):
                sbuf[n, 8 + 8 * m : 16 + 8 * m] = pm[pl.ds(16 + r, 8, stride=16), :]
        else:
            planes = (0,) if dx < 0 else (9, 10)
            for m, r in enumerate(planes):
                sbuf[n, 8 + 8 * m : 16 + 8 * m] = pm[pl.ds(16 * r + 8 * half, 8), :]

    pl.semaphore_wait(barrier, len(PEERS))

    fold = []
    for n, (dx, dy, dz) in enumerate(FOLD):
        if dz:
            side = 0 if dz > 0 else 1
            src = zbuf.at[side, int(dy != 0), int(dx != 0)]
            dst = rz.at[n]
        else:
            m = flat.index((dx, dy, dz))
            rows = 16 if (dx < 0 or (dx == 0 and dy < 0)) else 24
            src = sbuf.at[m, pl.ds(0, rows)]
            dst = r0.at[m, pl.ds(0, rows)]
        copy = pltpu.make_async_remote_copy(
            src_ref=src, dst_ref=dst, send_sem=send1.at[n], recv_sem=recv1.at[n],
            device_id=device_at(dx, dy, dz), device_id_type=MESH,
        )
        copy.start()
        fold.append(copy)

    def slopes(t, carry):
        zpos = z_position(t)
        ys[1, t] = bslope(y_distance(t))
        for c in range(ZROWS // 16):
            zz = zrow[pl.ds(16 * c, 16), :]
            u = jnp.concatenate([zz] * 4, axis=1) - zpos
            high, low = split(bslope(u))
            zsh[t, pl.ds(16 * c, 16), :] = high
            zsl[t, pl.ds(16 * c, 16), :] = low
        return carry

    lax.fori_loop(0, TILES, slopes, 0)

    for copy in fold:
        copy.wait_recv()

    row8 = lax.broadcasted_iota(jnp.int32, (8, 128), 0)
    lane8 = lax.broadcasted_iota(jnp.int32, (8, 128), 1)
    slot8 = lane8 // 16
    index8 = lane8 & 15

    def rows_of(dy, value):
        if dy == 0:
            return value
        return jnp.where((row8 < 2) if dy > 0 else (row8 == 7), value, 0.0)

    def slots_of(dx, value):
        if dx == 0:
            return value
        return jnp.where((slot8 < 2) if dx > 0 else (slot8 == 7), value, 0.0)

    low_end = jnp.zeros((8, 128), f32)
    high_end = jnp.zeros((8, 128), f32)
    own_end = ends[0][0:8]
    plane = [pm[pl.ds(16 * (x + 1), 8), :] for x in range(CX)]
    for n, (dx, dy, dz) in enumerate(FOLD):
        if dz > 0:
            low_end = low_end + slots_of(dx, rows_of(dy, rz[n]))
        elif dz < 0:
            high_end = high_end + slots_of(dx, rows_of(dy, rz[n]))
        else:
            m = flat.index((dx, dy, dz))
            own_end = own_end + slots_of(dx, rows_of(dy, r0[m, 0:8]))
            if dx > 0:
                plane[0] = plane[0] + rows_of(dy, r0[m, 8:16])
                plane[1] = plane[1] + rows_of(dy, r0[m, 16:24])
            elif dx < 0:
                plane[7] = plane[7] + rows_of(dy, r0[m, 8:16])
    for x in range(CX):
        down = pltpu.roll(low_end, (-(16 * x + 9)) % 128, 1)
        up = pltpu.roll(high_end, (127 - 16 * x) % 128, 1)
        add = jnp.where(lane8 < 2, down, jnp.where(lane8 == 127, up, 0.0))
        fm[pl.ds(8 * x, 8), :] = plane[x] + add
    after, before = flat.index((0, 1, 0)), flat.index((0, -1, 0))
    fm[pl.ds(7, 8, stride=8), :] += r0[before, 8:16]
    fm[pl.ds(0, 8, stride=8), :] += r0[after, 8:16]
    fm[pl.ds(1, 8, stride=8), :] += r0[after, 16:24]
    left = jnp.where(
        index8 < 8, low_end, jnp.where(index8 == 8, low_end + own_end, 0.0)
    )
    right = jnp.where((index8 == 1) | (index8 == 2), high_end + own_end, high_end)
    both_ends = jnp.concatenate([left, right], axis=0).astype(bf16)
    hb[0:16] = both_ends
    wrapped = jnp.where(lane8 < 64, pltpu.roll(right, 15, 1), pltpu.roll(left, 7, 1))
    hb[80:96] = jnp.concatenate([fm[pl.ds(56, 8), :], wrapped], axis=0).astype(bf16)
    for m in range(4):
        hb[16 + 16 * m : 32 + 16 * m] = fm[pl.ds(16 * m, 16), :].astype(bf16)

    halo = []
    for n, (dx, dy) in enumerate(HALO):
        start, rows = {2: (80, 16), -2: (0, 32)}.get(dx, (0, 80))
        copy = pltpu.make_async_remote_copy(
            src_ref=hb.at[pl.ds(start, rows)], dst_ref=rh.at[n, pl.ds(0, rows)],
            send_sem=send2.at[n], recv_sem=recv2.at[n],
            device_id=device_at(dx, dy, 0), device_id_type=MESH,
        )
        copy.start()
        halo.append(copy)

    xf[...] = jnp.zeros_like(xf)
    for i in range(SPAN):
        xf[32 * (i + 1) : 32 * (i + 1) + SPAN, 0:SPAN] = kern_ref[i].astype(f32)
    xb = xf[...].astype(bf16)
    eye = (
        lax.broadcasted_iota(jnp.int32, (24, 128), 0)
        == lax.broadcasted_iota(jnp.int32, (24, 128), 1)
    ).astype(f32).astype(bf16)
    blocks = []
    for h in range(2):
        kt = mm_nt(eye, xb[32 * (1 - h) : 32 * (1 - h) + 640])
        blocks += [kt[:, 128 * g : 128 * g + 128] for g in range(5)]
    lhs = jnp.concatenate(blocks, axis=0).astype(bf16)
    drow = lax.broadcasted_iota(jnp.int32, (128, 128), 0)
    dlane = lax.broadcasted_iota(jnp.int32, (128, 128), 1)
    base = (drow >> 6) * 64 + ((drow >> 5) & 1) * 8

    def shifted(n, carry):
        r = jnp.where(n < 10, n, 15)
        y = jnp.where(n < 10, n, -1)
        jy = ((drow & 31) + y) & 31
        target = base + (jy >> 3) * 16 + (jy & 7)
        sel = (dlane == target).astype(f32).astype(bf16)
        out = mm(lhs, sel)
        for h in range(2):
            for g in range(5):
                for c in range(3):
                    at = h * 120 + g * 24 + 8 * c
                    tf[g, pl.ds(h * 384 + 128 * c + r, 8, stride=16), :] = out[at : at + 8]
        return carry

    lax.fori_loop(0, 11, shifted, 0)
    for h in range(2):
        for g in range(5):
            for r in range(10, 15):
                for c in range(3):
                    tf[g, pl.ds(h * 384 + 128 * c + r, 8, stride=16), :] = jnp.zeros((8, 128), f32)
            tb[272 * h : 272 * h + 272, 128 * g : 128 * g + 128] = (
                tf[g, 384 * h : 384 * h + 272, :].astype(bf16)
            )

    def place(ends_bf16, main, xp, b, slots):
        at = xp * 64 + b * 16
        w[at : at + 16, 0:128] = main
        wide = ends_bf16.astype(f32)
        tops = []
        for s in slots:
            lo = pltpu.roll(wide[0:8], (119 - 16 * s) % 128, 1)
            hi = pltpu.roll(wide[8:16], (-1 - 16 * s) % 128, 1)
            tops.append(jnp.where(lane8 < 64, hi, lo))
        w[at : at + 16, 128:256] = jnp.concatenate(tops, axis=0).astype(bf16)

    for m in range(4):
        place(hb[0:16], hb[16 + 16 * m : 32 + 16 * m], 5 + m, 1, (2 * m, 2 * m + 1))
    for n in reversed(range(len(HALO))):
        dx, dy = HALO[n]
        halo[n].wait_recv()
        sx, b = -dx, (1 - dy) % 4
        if sx == 2:
            place(rh[n, 0:16], rh[n, 16:32], 13, b, (0, 1))
        elif sx == -2:
            last = rh[n, 0:16].astype(f32)
            blank = jnp.zeros((8, 128), f32)
            for half in range(2):
                w[16 * b : 16 * b + 16, 128 * half : 128 * half + 128] = jnp.concatenate(
                    [blank, last[8 * half : 8 * half + 8]], axis=0
                ).astype(bf16)
        else:
            for m in range(4):
                place(
                    rh[n, 0:16], rh[n, 16 + 16 * m : 32 + 16 * m],
                    4 * sx + 5 + m, b, (2 * m, 2 * m + 1),
                )

    for p in range(6):
        skip = 272 if p == 0 else 0
        out = mm(tb[skip:544, 0:576], w[64 * p : 64 * p + 576, :])
        for h in range(skip // 272, 2):
            acc = None
            for k in range(SPAN):
                at = 272 * h + 16 * k - skip
                term = out[at : at + 16]
                if k != 8:
                    term = pltpu.roll(term, (8 - k) % 256, 1)
                acc = term if acc is None else acc + term
            main, far = acc[:, 0:128], acc[:, 128:256]
            tail = jnp.where(
                (lane16 == 9) | (lane16 == 10),
                pltpu.roll(far, 9, 1),
                jnp.where(lane16 == 16, pltpu.roll(far, 17, 1), 0.0),
            )
            at = (2 * p + h) * 16
            mh, ml = split(main)
            th, tl = split(tail)
            phh[at : at + 16, 0:128] = mh
            phh[at : at + 16, 128:256] = th
            phl[at : at + 16, 0:128] = ml
            phl[at : at + 16, 128:256] = tl
            if 1 <= p <= 4:
                pot_ref[2 * p + h - 2] = main[0:8]

    for t in range(TILES):
        at = (t + 1) * 16
        high = phh[at : at + 64, 0:ZROWS]
        both = jnp.concatenate([high, phl[at : at + 64, 0:ZROWS]], axis=0)
        a = mm(both, zwh[t])
        value = a[:64] + a[64:] + mm(high, zwl[t])
        a = mm(both, zsh[t])
        slope = a[:64] + a[64:] + mm(high, zsl[t])
        fx = fy = fz = None
        for k in range(4):
            v, s = value[16 * k : 16 * k + 16], slope[16 * k : 16 * k + 16]
            wx, sx = xs[k, t : t + 1, :], xs[4 + k, t : t + 1, :]
            ax, ay, az = sx * v, wx * v, wx * s
            fx = ax if fx is None else fx + ax
            fy = ay if fy is None else fy + ay
            fz = az if fz is None else fz + az
        wy, sy = ys[0, t], ys[1, t]
        frc_ref[0, t, 0] = jnp.sum(fx * wy, axis=0, keepdims=True)
        frc_ref[1, t, 0] = -jnp.sum(fy * sy, axis=0, keepdims=True)
        frc_ref[2, t, 0] = -jnp.sum(fz * wy, axis=0, keepdims=True)

    for copy in fold:
        copy.wait_send()
    for copy in halo:
        copy.wait_send()


def local(charges, offsets, cells, kernel):
    f32, bf16 = jnp.float32, jnp.bfloat16
    vmem = pl.BlockSpec(memory_space=pltpu.VMEM)
    return pl.pallas_call(
        body,
        out_shape=(
            jax.ShapeDtypeStruct((CX, CY, CZ), f32),
            jax.ShapeDtypeStruct((3, TILES, 1, 1, APT), f32),
        ),
        in_specs=[pl.BlockSpec(memory_space=pltpu.HBM)] * 4,
        out_specs=(vmem, vmem),
        scratch_shapes=[
            pltpu.VMEM((TILES, APT), f32),
            pltpu.VMEM((3, TILES, APT), f32),
            pltpu.VMEM((2, TILES, APT), jnp.int32),
            pltpu.VMEM((SPAN, SPAN, SPAN), bf16),
            pltpu.VMEM((2, TILES, 16, APT), f32),
            pltpu.VMEM((8, TILES, APT), f32),
            pltpu.VMEM((ZROWS, 128), f32),
            pltpu.VMEM((TILES, ZROWS, APT), bf16),
            pltpu.VMEM((TILES, ZROWS, APT), bf16),
            pltpu.VMEM((TILES, ZROWS, APT), bf16),
            pltpu.VMEM((TILES, ZROWS, APT), bf16),
            pltpu.VMEM((16 * (CX + 3), 128), f32),
            pltpu.VMEM((16 * (CX + 3), 128), f32),
            pltpu.VMEM((2, 2, 2, 8, 128), f32),
            pltpu.VMEM((8, 24, 128), f32),
            pltpu.VMEM((len(FOLD), 8, 128), f32),
            pltpu.VMEM((8, 24, 128), f32),
            pltpu.VMEM((64, 128), f32),
            pltpu.VMEM((96, 128), bf16),
            pltpu.VMEM((len(HALO), 80, 128), bf16),
            pltpu.VMEM((32 * 21, 128), f32),
            pltpu.VMEM((5, 768, 128), f32),
            pltpu.VMEM((544, 640), bf16),
            pltpu.VMEM((14 * 64, 256), bf16),
            pltpu.VMEM((192, 256), bf16),
            pltpu.VMEM((192, 256), bf16),
            pltpu.SemaphoreType.DMA((4,)),
            pltpu.SemaphoreType.DMA((len(FOLD),)),
            pltpu.SemaphoreType.DMA((len(FOLD),)),
            pltpu.SemaphoreType.DMA((len(HALO),)),
            pltpu.SemaphoreType.DMA((len(HALO),)),
        ],
        compiler_params=pltpu.CompilerParams(
            collective_id=0, has_side_effects=True, vmem_limit_bytes=64 * 1024 * 1024
        ),
    )(charges, offsets, cells, kernel)


def solution(mesh):
    placed = (
        P("gx", "gy", "gz", None),
        P(None, "gx", "gy", "gz", None),
        P(None, "gx", "gy", "gz", None),
        P(),
    )
    return jax.shard_map(
        local,
        mesh=mesh,
        in_specs=placed,
        out_specs=(P("gx", "gy", "gz"), P(None, "gx", "gy", "gz", None)),
        check_vma=False,
    )
```

```python
import jax
import jax.numpy as jnp
from jax import lax
from jax.experimental import pallas as pl
from jax.experimental.pallas import tpu as pltpu
from jax.sharding import PartitionSpec as P

CX = 8
CY = 8
CZ = 128
TILES = 8
APT = 512
SPAN = 17
ZROWS = 160
MESH = pl.DeviceIdType.MESH

FOLD = [
    (dx, dy, dz)
    for dx in (1, 0, -1)
    for dy, dz in ((1, 1), (-1, 1), (1, -1), (-1, -1), (0, 1), (0, -1), (1, 0), (-1, 0), (0, 0))
    if (dx, dy, dz) != (0, 0, 0)
]
HALO = [(dx, dy) for dy in (2, 1, -1, 0) for dx in (2, 1)]
HALO += [(0, dy) for dy in (2, 1, -1)]
HALO += [(dx, dy) for dy in (2, 1, -1, 0) for dx in (-2, -1)]
PEERS = FOLD


def neighbours():
    tables = []
    for axis in ("gx", "gy", "gz"):
        size = lax.axis_size(axis)
        index = lax.axis_index(axis)
        table = {0: index}
        for step in (1, 2):
            up, down = index + step, index - step
            table[step] = jnp.where(up >= size, up - size, up)
            table[-step] = jnp.where(down < 0, down + size, down)
        table[3] = table[-1]
        tables.append(table)
    return lambda dx, dy, dz: (tables[0][dx], tables[1][dy], tables[2][dz])


def x_splines(f):
    r = 1.0 - f
    values = [
        r * r * r / 6.0,
        (3.0 * f * f * f - 6.0 * f * f + 4.0) / 6.0,
        (-3.0 * f * f * f + 3.0 * f * f + 3.0 * f + 1.0) / 6.0,
        f * f * f / 6.0,
    ]
    slopes = [-0.5 * r * r, 1.5 * f * f - 2.0 * f, -1.5 * f * f + f + 0.5, 0.5 * f * f]
    return values, slopes


def bspline(u):
    a = jnp.abs(u)
    p = jnp.maximum(2.0 - a, 0.0)
    q = jnp.maximum(1.0 - a, 0.0)
    return p * p * p * (1.0 / 6.0) - q * q * q * (2.0 / 3.0)


def bslope(u):
    a = jnp.abs(u)
    p = jnp.maximum(2.0 - a, 0.0)
    q = jnp.maximum(1.0 - a, 0.0)
    m = 0.5 * p * p - 2.0 * q * q
    return jnp.where(u < 0.0, -m, m)


def split(value):
    high = value.astype(jnp.bfloat16)
    low = (value - high.astype(jnp.float32)).astype(jnp.bfloat16)
    return high, low


def mm(a, b):
    return jnp.dot(a, b, preferred_element_type=jnp.float32)


def mm_nt(a, b):
    return lax.dot_general(a, b, (((1,), (1,)), ((), ())), preferred_element_type=jnp.float32)


def body(
    q_hbm, off_hbm, cell_hbm, kern_hbm, pot_ref, frc_ref,
    q_ref, off_ref, cell_ref, kern_ref, ys, xs,
    zrow, zwh, zwl, zsh, zsl, pm, pe, zbuf, sbuf, rz, r0, fm, hb, rh,
    xf, tf, tb, w, phh, phl, load, send1, recv1, send2, recv2,
):
    iy = lax.axis_index("gy")
    iz = lax.axis_index("gz")
    f32, bf16 = jnp.float32, jnp.bfloat16

    device_at = neighbours()
    barrier = pltpu.get_barrier_semaphore()
    for peer in PEERS:
        pl.semaphore_signal(barrier, inc=1, device_id=device_at(*peer), device_id_type=MESH)

    loads = [
        pltpu.make_async_copy(q_hbm.at[:, 0, 0, :], q_ref, load.at[0]),
        pltpu.make_async_copy(off_hbm.at[:, :, 0, 0, :], off_ref, load.at[1]),
        pltpu.make_async_copy(cell_hbm.at[:, :, 0, 0, :], cell_ref, load.at[2]),
        pltpu.make_async_copy(kern_hbm, kern_ref, load.at[3]),
    ]
    for copy in loads:
        copy.start()

    row_id = lax.broadcasted_iota(jnp.int32, (ZROWS, 128), 0)
    zrow[...] = jnp.where(
        row_id < 128, row_id, jnp.where(row_id < 144, row_id - 9, row_id - 145)
    ).astype(f32)
    pm[...] = jnp.zeros_like(pm)
    pe[...] = jnp.zeros_like(pe)
    y_id = lax.broadcasted_iota(jnp.int32, (16, APT), 0)
    y_id = jnp.where(y_id < 15, y_id, -1).astype(f32)

    def y_distance(t):
        ly = (cell_ref[0, pl.ds(t, 1), :] - iy * CY).astype(f32)
        return (y_id - ly) - off_ref[1, pl.ds(t, 1), :]

    def z_position(t):
        return (cell_ref[1, pl.ds(t, 1), :] - iz * CZ).astype(f32) + off_ref[2, pl.ds(t, 1), :]

    for copy in loads:
        copy.wait()
    values, derivatives = x_splines(off_ref[0])
    for k in range(4):
        xs[k] = q_ref[...] * values[k]
        xs[4 + k] = -q_ref[...] * derivatives[k]

    def spread(t, carry):
        zpos = z_position(t)
        for c in range(ZROWS // 16):
            zz = zrow[pl.ds(16 * c, 16), :]
            u = jnp.concatenate([zz] * 4, axis=1) - zpos
            high, low = split(bspline(u))
            zwh[t, pl.ds(16 * c, 16), :] = high
            zwl[t, pl.ds(16 * c, 16), :] = low
        wy = bspline(y_distance(t))
        ys[0, t] = wy
        parts = [split(xs[k, pl.ds(t, 1), :] * wy) for k in range(4)]
        high = jnp.concatenate([p[0] for p in parts], axis=0)
        both = jnp.concatenate([high] + [p[1] for p in parts], axis=0)
        first = mm_nt(both, zwh[t])
        total = first[:64] + first[64:] + mm_nt(high, zwl[t])
        for k in range(4):
            at = pl.multiple_of((t + k) * 16, 16)
            pm[pl.ds(at, 16), :] += total[16 * k : 16 * k + 16, :128]
            pe[pl.ds(at, 16), 0:32] += total[16 * k : 16 * k + 16, 128:160]
        return carry

    lax.fori_loop(0, TILES, spread, 0, unroll=2)

    lane16 = lax.broadcasted_iota(jnp.int32, (16, 128), 1)
    index16 = lane16 & 15
    zero16 = jnp.zeros((16, 128), f32)
    zr = [zero16, zero16]
    zl = [zero16, zero16]
    for n in range(CX + 3):
        x = n - 1
        part, slot = (0, x) if 0 <= x < 8 else (1, x % 8)
        e = pe[pl.ds(16 * n, 16), :]
        er = jnp.where(lane16 < 16, e, 0.0)
        el = jnp.where((lane16 >= 16) & (lane16 < 32), e, 0.0)
        zr[part] = zr[part] + pltpu.roll(er, 16 * slot, 1)
        zl[part] = zl[part] + pltpu.roll(el, (16 * slot + 112) % 128, 1)
    ends = []
    for part in range(2):
        ends.append(
            jnp.where(
                (index16 == 1) | (index16 == 2),
                pltpu.roll(zr[part], 120, 1),
                jnp.where(index16 == 8, pltpu.roll(zl[part], 8, 1), 0.0),
            )
        )
        for half in range(2):
            zbuf[0, half, part] = zr[part][8 * half : 8 * half + 8]
            zbuf[1, half, part] = zl[part][8 * half : 8 * half + 8]
    flat = [m for m in FOLD if m[2] == 0]
    for n, (dx, dy, _) in enumerate(flat):
        half, part = int(dy != 0), int(dx != 0)
        sbuf[n, 0:8] = ends[part][8 * half : 8 * half + 8]
        if dx == 0:
            rows = (15,) if dy < 0 else (8, 9)
            for m, r in enumerate(rows):
                sbuf[n, 8 + 8 * m : 16 + 8 * m] = pm[pl.ds(16 + r, 8, stride=16), :]
        else:
            planes = (0,) if dx < 0 else (9, 10)
            for m, r in enumerate(planes):
                sbuf[n, 8 + 8 * m : 16 + 8 * m] = pm[pl.ds(16 * r + 8 * half, 8), :]

    pl.semaphore_wait(barrier, len(PEERS))

    fold = []
    for n, (dx, dy, dz) in enumerate(FOLD):
        if dz:
            side = 0 if dz > 0 else 1
            src = zbuf.at[side, int(dy != 0), int(dx != 0)]
            dst = rz.at[n]
        else:
            m = flat.index((dx, dy, dz))
            rows = 16 if (dx < 0 or (dx == 0 and dy < 0)) else 24
            src = sbuf.at[m, pl.ds(0, rows)]
            dst = r0.at[m, pl.ds(0, rows)]
        copy = pltpu.make_async_remote_copy(
            src_ref=src, dst_ref=dst, send_sem=send1.at[n], recv_sem=recv1.at[n],
            device_id=device_at(dx, dy, dz), device_id_type=MESH,
        )
        copy.start()
        fold.append(copy)

    def slopes(t, carry):
        zpos = z_position(t)
        ys[1, t] = bslope(y_distance(t))
        for c in range(ZROWS // 16):
            zz = zrow[pl.ds(16 * c, 16), :]
            u = jnp.concatenate([zz] * 4, axis=1) - zpos
            high, low = split(bslope(u))
            zsh[t, pl.ds(16 * c, 16), :] = high
            zsl[t, pl.ds(16 * c, 16), :] = low
        return carry

    lax.fori_loop(0, TILES, slopes, 0)

    for copy in fold:
        copy.wait_recv()

    row8 = lax.broadcasted_iota(jnp.int32, (8, 128), 0)
    lane8 = lax.broadcasted_iota(jnp.int32, (8, 128), 1)
    slot8 = lane8 // 16
    index8 = lane8 & 15

    def rows_of(dy, value):
        if dy == 0:
            return value
        return jnp.where((row8 < 2) if dy > 0 else (row8 == 7), value, 0.0)

    def slots_of(dx, value):
        if dx == 0:
            return value
        return jnp.where((slot8 < 2) if dx > 0 else (slot8 == 7), value, 0.0)

    low_end = jnp.zeros((8, 128), f32)
    high_end = jnp.zeros((8, 128), f32)
    own_end = ends[0][0:8]
    plane = [pm[pl.ds(16 * (x + 1), 8), :] for x in range(CX)]
    for n, (dx, dy, dz) in enumerate(FOLD):
        if dz > 0:
            low_end = low_end + slots_of(dx, rows_of(dy, rz[n]))
        elif dz < 0:
            high_end = high_end + slots_of(dx, rows_of(dy, rz[n]))
        else:
            m = flat.index((dx, dy, dz))
            own_end = own_end + slots_of(dx, rows_of(dy, r0[m, 0:8]))
            if dx > 0:
                plane[0] = plane[0] + rows_of(dy, r0[m, 8:16])
                plane[1] = plane[1] + rows_of(dy, r0[m, 16:24])
            elif dx < 0:
                plane[7] = plane[7] + rows_of(dy, r0[m, 8:16])
    for x in range(CX):
        down = pltpu.roll(low_end, (-(16 * x + 9)) % 128, 1)
        up = pltpu.roll(high_end, (127 - 16 * x) % 128, 1)
        add = jnp.where(lane8 < 2, down, jnp.where(lane8 == 127, up, 0.0))
        fm[pl.ds(8 * x, 8), :] = plane[x] + add
    after, before = flat.index((0, 1, 0)), flat.index((0, -1, 0))
    fm[pl.ds(7, 8, stride=8), :] += r0[before, 8:16]
    fm[pl.ds(0, 8, stride=8), :] += r0[after, 8:16]
    fm[pl.ds(1, 8, stride=8), :] += r0[after, 16:24]
    left = jnp.where(
        index8 < 8, low_end, jnp.where(index8 == 8, low_end + own_end, 0.0)
    )
    right = jnp.where((index8 == 1) | (index8 == 2), high_end + own_end, high_end)
    both_ends = jnp.concatenate([left, right], axis=0).astype(bf16)
    hb[0:16] = both_ends
    wrapped = jnp.where(lane8 < 64, pltpu.roll(right, 15, 1), pltpu.roll(left, 7, 1))
    hb[80:96] = jnp.concatenate([fm[pl.ds(56, 8), :], wrapped], axis=0).astype(bf16)
    for m in range(4):
        hb[16 + 16 * m : 32 + 16 * m] = fm[pl.ds(16 * m, 16), :].astype(bf16)

    halo = []
    for n, (dx, dy) in enumerate(HALO):
        start, rows = {2: (80, 16), -2: (0, 32)}.get(dx, (0, 80))
        copy = pltpu.make_async_remote_copy(
            src_ref=hb.at[pl.ds(start, rows)], dst_ref=rh.at[n, pl.ds(0, rows)],
            send_sem=send2.at[n], recv_sem=recv2.at[n],
            device_id=device_at(dx, dy, 0), device_id_type=MESH,
        )
        copy.start()
        halo.append(copy)

    xf[...] = jnp.zeros_like(xf)
    for i in range(SPAN):
        xf[32 * (i + 1) : 32 * (i + 1) + SPAN, 0:SPAN] = kern_ref[i].astype(f32)
    xb = xf[...].astype(bf16)
    eye = (
        lax.broadcasted_iota(jnp.int32, (24, 128), 0)
        == lax.broadcasted_iota(jnp.int32, (24, 128), 1)
    ).astype(f32).astype(bf16)
    blocks = []
    for h in range(2):
        kt = mm_nt(eye, xb[32 * (1 - h) : 32 * (1 - h) + 640])
        blocks += [kt[:, 128 * g : 128 * g + 128] for g in range(5)]
    lhs = jnp.concatenate(blocks, axis=0).astype(bf16)
    drow = lax.broadcasted_iota(jnp.int32, (128, 128), 0)
    dlane = lax.broadcasted_iota(jnp.int32, (128, 128), 1)
    base = (drow >> 6) * 64 + ((drow >> 5) & 1) * 8

    def shifted(n, carry):
        r = jnp.where(n < 10, n, 15)
        y = jnp.where(n < 10, n, -1)
        jy = ((drow & 31) + y) & 31
        target = base + (jy >> 3) * 16 + (jy & 7)
        sel = (dlane == target).astype(f32).astype(bf16)
        out = mm(lhs, sel)
        for h in range(2):
            for g in range(5):
                for c in range(3):
                    at = h * 120 + g * 24 + 8 * c
                    tf[g, pl.ds(h * 384 + 128 * c + r, 8, stride=16), :] = out[at : at + 8]
        return carry

    lax.fori_loop(0, 11, shifted, 0)
    for h in range(2):
        for g in range(5):
            for r in range(10, 15):
                for c in range(3):
                    tf[g, pl.ds(h * 384 + 128 * c + r, 8, stride=16), :] = jnp.zeros((8, 128), f32)
            tb[272 * h : 272 * h + 272, 128 * g : 128 * g + 128] = (
                tf[g, 384 * h : 384 * h + 272, :].astype(bf16)
            )

    def place(ends_bf16, main, xp, b, slots):
        at = xp * 64 + b * 16
        w[at : at + 16, 0:128] = main
        wide = ends_bf16.astype(f32)
        tops = []
        for s in slots:
            lo = pltpu.roll(wide[0:8], (119 - 16 * s) % 128, 1)
            hi = pltpu.roll(wide[8:16], (-1 - 16 * s) % 128, 1)
            tops.append(jnp.where(lane8 < 64, hi, lo))
        w[at : at + 16, 128:256] = jnp.concatenate(tops, axis=0).astype(bf16)

    for m in range(4):
        place(hb[0:16], hb[16 + 16 * m : 32 + 16 * m], 5 + m, 1, (2 * m, 2 * m + 1))
    for n in reversed(range(len(HALO))):
        dx, dy = HALO[n]
        halo[n].wait_recv()
        sx, b = -dx, (1 - dy) % 4
        if sx == 2:
            place(rh[n, 0:16], rh[n, 16:32], 13, b, (0, 1))
        elif sx == -2:
            last = rh[n, 0:16].astype(f32)
            blank = jnp.zeros((8, 128), f32)
            for half in range(2):
                w[16 * b : 16 * b + 16, 128 * half : 128 * half + 128] = jnp.concatenate(
                    [blank, last[8 * half : 8 * half + 8]], axis=0
                ).astype(bf16)
        else:
            for m in range(4):
                place(
                    rh[n, 0:16], rh[n, 16 + 16 * m : 32 + 16 * m],
                    4 * sx + 5 + m, b, (2 * m, 2 * m + 1),
                )

    for p in range(6):
        skip = 272 if p == 0 else 0
        out = mm(tb[skip:544, 0:576], w[64 * p : 64 * p + 576, :])
        for h in range(skip // 272, 2):
            acc = None
            for k in range(SPAN):
                at = 272 * h + 16 * k - skip
                term = out[at : at + 16]
                if k != 8:
                    term = pltpu.roll(term, (8 - k) % 256, 1)
                acc = term if acc is None else acc + term
            main, far = acc[:, 0:128], acc[:, 128:256]
            tail = jnp.where(
                (lane16 == 9) | (lane16 == 10),
                pltpu.roll(far, 9, 1),
                jnp.where(lane16 == 16, pltpu.roll(far, 17, 1), 0.0),
            )
            at = (2 * p + h) * 16
            mh, ml = split(main)
            th, tl = split(tail)
            phh[at : at + 16, 0:128] = mh
            phh[at : at + 16, 128:256] = th
            phl[at : at + 16, 0:128] = ml
            phl[at : at + 16, 128:256] = tl
            if 1 <= p <= 4:
                pot_ref[2 * p + h - 2] = main[0:8]

    for t in range(TILES):
        at = (t + 1) * 16
        high = phh[at : at + 64, 0:ZROWS]
        both = jnp.concatenate([high, phl[at : at + 64, 0:ZROWS]], axis=0)
        a = mm(both, zwh[t])
        value = a[:64] + a[64:] + mm(high, zwl[t])
        a = mm(both, zsh[t])
        slope = a[:64] + a[64:] + mm(high, zsl[t])
        fx = fy = fz = None
        for k in range(4):
            v, s = value[16 * k : 16 * k + 16], slope[16 * k : 16 * k + 16]
            wx, sx = xs[k, t : t + 1, :], xs[4 + k, t : t + 1, :]
            ax, ay, az = sx * v, wx * v, wx * s
            fx = ax if fx is None else fx + ax
            fy = ay if fy is None else fy + ay
            fz = az if fz is None else fz + az
        wy, sy = ys[0, t], ys[1, t]
        frc_ref[0, t, 0] = jnp.sum(fx * wy, axis=0, keepdims=True)
        frc_ref[1, t, 0] = -jnp.sum(fy * sy, axis=0, keepdims=True)
        frc_ref[2, t, 0] = -jnp.sum(fz * wy, axis=0, keepdims=True)

    for copy in fold:
        copy.wait_send()
    for copy in halo:
        copy.wait_send()


def local(charges, offsets, cells, kernel):
    f32, bf16 = jnp.float32, jnp.bfloat16
    vmem = pl.BlockSpec(memory_space=pltpu.VMEM)
    return pl.pallas_call(
        body,
        out_shape=(
            pltpu.VMEM((CX, CY, CZ), f32),
            pltpu.VMEM((3, TILES, 1, 1, APT), f32),
        ),
        in_specs=[pl.BlockSpec(memory_space=pltpu.HBM)] * 4,
        out_specs=(vmem, vmem),
        scratch_shapes=[
            pltpu.VMEM((TILES, APT), f32),
            pltpu.VMEM((3, TILES, APT), f32),
            pltpu.VMEM((2, TILES, APT), jnp.int32),
            pltpu.VMEM((SPAN, SPAN, SPAN), bf16),
            pltpu.VMEM((2, TILES, 16, APT), f32),
            pltpu.VMEM((8, TILES, APT), f32),
            pltpu.VMEM((ZROWS, 128), f32),
            pltpu.VMEM((TILES, ZROWS, APT), bf16),
            pltpu.VMEM((TILES, ZROWS, APT), bf16),
            pltpu.VMEM((TILES, ZROWS, APT), bf16),
            pltpu.VMEM((TILES, ZROWS, APT), bf16),
            pltpu.VMEM((16 * (CX + 3), 128), f32),
            pltpu.VMEM((16 * (CX + 3), 128), f32),
            pltpu.VMEM((2, 2, 2, 8, 128), f32),
            pltpu.VMEM((8, 24, 128), f32),
            pltpu.VMEM((len(FOLD), 8, 128), f32),
            pltpu.VMEM((8, 24, 128), f32),
            pltpu.VMEM((64, 128), f32),
            pltpu.VMEM((96, 128), bf16),
            pltpu.VMEM((len(HALO), 80, 128), bf16),
            pltpu.VMEM((32 * 21, 128), f32),
            pltpu.VMEM((5, 768, 128), f32),
            pltpu.VMEM((544, 640), bf16),
            pltpu.VMEM((14 * 64, 256), bf16),
            pltpu.VMEM((192, 256), bf16),
            pltpu.VMEM((192, 256), bf16),
            pltpu.SemaphoreType.DMA((4,)),
            pltpu.SemaphoreType.DMA((len(FOLD),)),
            pltpu.SemaphoreType.DMA((len(FOLD),)),
            pltpu.SemaphoreType.DMA((len(HALO),)),
            pltpu.SemaphoreType.DMA((len(HALO),)),
        ],
        compiler_params=pltpu.CompilerParams(
            collective_id=0, has_side_effects=True, vmem_limit_bytes=60 * 1024 * 1024
        ),
    )(charges, offsets, cells, kernel)


def solution(mesh):
    placed = (
        P("gx", "gy", "gz", None),
        P(None, "gx", "gy", "gz", None),
        P(None, "gx", "gy", "gz", None),
        P(),
    )
    return jax.shard_map(
        local,
        mesh=mesh,
        in_specs=placed,
        out_specs=(P("gx", "gy", "gz"), P(None, "gx", "gy", "gz", None)),
        check_vma=False,
    )
```

```python
import jax
import jax.numpy as jnp
from jax import lax
from jax.experimental import pallas as pl
from jax.experimental.pallas import tpu as pltpu
from jax.sharding import PartitionSpec as P

CX = 8
CY = 8
CZ = 128
TILES = 8
APT = 512
SPAN = 17
ZROWS = 160
MESH = pl.DeviceIdType.MESH

FOLD = [
    (dx, dy, dz)
    for dx in (1, 0, -1)
    for dy, dz in ((1, 1), (-1, 1), (1, -1), (-1, -1), (0, 1), (0, -1), (1, 0), (-1, 0), (0, 0))
    if (dx, dy, dz) != (0, 0, 0)
]
HALO = [(dx, dy) for dy in (2, 1, -1, 0) for dx in (2, 1)]
HALO += [(0, dy) for dy in (2, 1, -1)]
HALO += [(dx, dy) for dy in (2, 1, -1, 0) for dx in (-2, -1)]
PEERS = FOLD


def neighbours():
    tables = []
    for axis in ("gx", "gy", "gz"):
        size = lax.axis_size(axis)
        index = lax.axis_index(axis)
        table = {0: index}
        for step in (1, 2):
            up, down = index + step, index - step
            table[step] = jnp.where(up >= size, up - size, up)
            table[-step] = jnp.where(down < 0, down + size, down)
        table[3] = table[-1]
        tables.append(table)
    return lambda dx, dy, dz: (tables[0][dx], tables[1][dy], tables[2][dz])


def x_splines(f):
    r = 1.0 - f
    values = [
        r * r * r / 6.0,
        (3.0 * f * f * f - 6.0 * f * f + 4.0) / 6.0,
        (-3.0 * f * f * f + 3.0 * f * f + 3.0 * f + 1.0) / 6.0,
        f * f * f / 6.0,
    ]
    slopes = [-0.5 * r * r, 1.5 * f * f - 2.0 * f, -1.5 * f * f + f + 0.5, 0.5 * f * f]
    return values, slopes


def bspline(u):
    a = jnp.abs(u)
    p = jnp.maximum(2.0 - a, 0.0)
    q = jnp.maximum(1.0 - a, 0.0)
    return p * p * p * (1.0 / 6.0) - q * q * q * (2.0 / 3.0)


def bslope(u):
    a = jnp.abs(u)
    p = jnp.maximum(2.0 - a, 0.0)
    q = jnp.maximum(1.0 - a, 0.0)
    m = 0.5 * p * p - 2.0 * q * q
    return jnp.where(u < 0.0, -m, m)


def split(value):
    high = value.astype(jnp.bfloat16)
    low = (value - high.astype(jnp.float32)).astype(jnp.bfloat16)
    return high, low


def mm(a, b):
    return jnp.dot(a, b, preferred_element_type=jnp.float32)


def mm_nt(a, b):
    return lax.dot_general(a, b, (((1,), (1,)), ((), ())), preferred_element_type=jnp.float32)


def body(
    q_hbm, off_hbm, cell_hbm, kern_hbm, pot_ref, frc_ref,
    q_ref, off_ref, cell_ref, kern_ref, ys, xs,
    zrow, zwh, zwl, zsh, zsl, pm, pe, zbuf, sbuf, rz, r0, fm, hb, rh,
    xf, tf, tb, w, phh, phl, load, send1, recv1, send2, recv2,
):
    iy = lax.axis_index("gy")
    iz = lax.axis_index("gz")
    f32, bf16 = jnp.float32, jnp.bfloat16

    device_at = neighbours()
    barrier = pltpu.get_barrier_semaphore()
    for peer in PEERS:
        pl.semaphore_signal(barrier, inc=1, device_id=device_at(*peer), device_id_type=MESH)

    loads = [
        pltpu.make_async_copy(q_hbm.at[:, 0, 0, :], q_ref, load.at[0]),
        pltpu.make_async_copy(off_hbm.at[:, :, 0, 0, :], off_ref, load.at[1]),
        pltpu.make_async_copy(cell_hbm.at[:, :, 0, 0, :], cell_ref, load.at[2]),
        pltpu.make_async_copy(kern_hbm, kern_ref, load.at[3]),
    ]
    for copy in loads:
        copy.start()

    row_id = lax.broadcasted_iota(jnp.int32, (ZROWS, 128), 0)
    zrow[...] = jnp.where(
        row_id < 128, row_id, jnp.where(row_id < 144, row_id - 9, row_id - 145)
    ).astype(f32)
    pm[...] = jnp.zeros_like(pm)
    pe[...] = jnp.zeros_like(pe)
    y_id = lax.broadcasted_iota(jnp.int32, (16, APT), 0)
    y_id = jnp.where(y_id < 15, y_id, -1).astype(f32)

    def y_distance(t):
        ly = (cell_ref[0, pl.ds(t, 1), :] - iy * CY).astype(f32)
        return (y_id - ly) - off_ref[1, pl.ds(t, 1), :]

    def z_position(t):
        return (cell_ref[1, pl.ds(t, 1), :] - iz * CZ).astype(f32) + off_ref[2, pl.ds(t, 1), :]

    for copy in loads:
        copy.wait()
    values, derivatives = x_splines(off_ref[0])
    for k in range(4):
        xs[k] = q_ref[...] * values[k]
        xs[4 + k] = -q_ref[...] * derivatives[k]

    def spread(t, carry):
        zpos = z_position(t)
        for c in range(ZROWS // 16):
            zz = zrow[pl.ds(16 * c, 16), :]
            u = jnp.concatenate([zz] * 4, axis=1) - zpos
            high, low = split(bspline(u))
            zwh[t, pl.ds(16 * c, 16), :] = high
            zwl[t, pl.ds(16 * c, 16), :] = low
        wy = bspline(y_distance(t))
        ys[0, t] = wy
        parts = [split(xs[k, pl.ds(t, 1), :] * wy) for k in range(4)]
        high = jnp.concatenate([p[0] for p in parts], axis=0)
        both = jnp.concatenate([high] + [p[1] for p in parts], axis=0)
        first = mm_nt(both, zwh[t])
        total = first[:64] + first[64:] + mm_nt(high, zwl[t])
        for k in range(4):
            at = pl.multiple_of((t + k) * 16, 16)
            pm[pl.ds(at, 16), :] += total[16 * k : 16 * k + 16, :128]
            pe[pl.ds(at, 16), 0:32] += total[16 * k : 16 * k + 16, 128:160]
        return carry

    lax.fori_loop(0, TILES, spread, 0, unroll=2)

    lane16 = lax.broadcasted_iota(jnp.int32, (16, 128), 1)
    index16 = lane16 & 15
    zero16 = jnp.zeros((16, 128), f32)
    zr = [zero16, zero16]
    zl = [zero16, zero16]
    for n in range(CX + 3):
        x = n - 1
        part, slot = (0, x) if 0 <= x < 8 else (1, x % 8)
        e = pe[pl.ds(16 * n, 16), :]
        er = jnp.where(lane16 < 16, e, 0.0)
        el = jnp.where((lane16 >= 16) & (lane16 < 32), e, 0.0)
        zr[part] = zr[part] + pltpu.roll(er, 16 * slot, 1)
        zl[part] = zl[part] + pltpu.roll(el, (16 * slot + 112) % 128, 1)
    ends = []
    for part in range(2):
        ends.append(
            jnp.where(
                (index16 == 1) | (index16 == 2),
                pltpu.roll(zr[part], 120, 1),
                jnp.where(index16 == 8, pltpu.roll(zl[part], 8, 1), 0.0),
            )
        )
        for half in range(2):
            zbuf[0, half, part] = zr[part][8 * half : 8 * half + 8]
            zbuf[1, half, part] = zl[part][8 * half : 8 * half + 8]
    flat = [m for m in FOLD if m[2] == 0]
    for n, (dx, dy, _) in enumerate(flat):
        half, part = int(dy != 0), int(dx != 0)
        sbuf[n, 0:8] = ends[part][8 * half : 8 * half + 8]
        if dx == 0:
            rows = (15,) if dy < 0 else (8, 9)
            for m, r in enumerate(rows):
                sbuf[n, 8 + 8 * m : 16 + 8 * m] = pm[pl.ds(16 + r, 8, stride=16), :]
        else:
            planes = (0,) if dx < 0 else (9, 10)
            for m, r in enumerate(planes):
                sbuf[n, 8 + 8 * m : 16 + 8 * m] = pm[pl.ds(16 * r + 8 * half, 8), :]

    pl.semaphore_wait(barrier, len(PEERS))

    fold = []
    for n, (dx, dy, dz) in enumerate(FOLD):
        if dz:
            side = 0 if dz > 0 else 1
            src = zbuf.at[side, int(dy != 0), int(dx != 0)]
            dst = rz.at[n]
        else:
            m = flat.index((dx, dy, dz))
            rows = 16 if (dx < 0 or (dx == 0 and dy < 0)) else 24
            src = sbuf.at[m, pl.ds(0, rows)]
            dst = r0.at[m, pl.ds(0, rows)]
        copy = pltpu.make_async_remote_copy(
            src_ref=src, dst_ref=dst, send_sem=send1.at[n], recv_sem=recv1.at[n],
            device_id=device_at(dx, dy, dz), device_id_type=MESH,
        )
        copy.start()
        fold.append(copy)

    def slopes(t, carry):
        zpos = z_position(t)
        ys[1, t] = bslope(y_distance(t))
        for c in range(ZROWS // 16):
            zz = zrow[pl.ds(16 * c, 16), :]
            u = jnp.concatenate([zz] * 4, axis=1) - zpos
            high, low = split(bslope(u))
            zsh[t, pl.ds(16 * c, 16), :] = high
            zsl[t, pl.ds(16 * c, 16), :] = low
        return carry

    lax.fori_loop(0, TILES, slopes, 0)

    for copy in fold:
        copy.wait_recv()

    row8 = lax.broadcasted_iota(jnp.int32, (8, 128), 0)
    lane8 = lax.broadcasted_iota(jnp.int32, (8, 128), 1)
    slot8 = lane8 // 16
    index8 = lane8 & 15

    def rows_of(dy, value):
        if dy == 0:
            return value
        return jnp.where((row8 < 2) if dy > 0 else (row8 == 7), value, 0.0)

    def slots_of(dx, value):
        if dx == 0:
            return value
        return jnp.where((slot8 < 2) if dx > 0 else (slot8 == 7), value, 0.0)

    low_end = jnp.zeros((8, 128), f32)
    high_end = jnp.zeros((8, 128), f32)
    own_end = ends[0][0:8]
    plane = [pm[pl.ds(16 * (x + 1), 8), :] for x in range(CX)]
    for n, (dx, dy, dz) in enumerate(FOLD):
        if dz > 0:
            low_end = low_end + slots_of(dx, rows_of(dy, rz[n]))
        elif dz < 0:
            high_end = high_end + slots_of(dx, rows_of(dy, rz[n]))
        else:
            m = flat.index((dx, dy, dz))
            own_end = own_end + slots_of(dx, rows_of(dy, r0[m, 0:8]))
            if dx > 0:
                plane[0] = plane[0] + rows_of(dy, r0[m, 8:16])
                plane[1] = plane[1] + rows_of(dy, r0[m, 16:24])
            elif dx < 0:
                plane[7] = plane[7] + rows_of(dy, r0[m, 8:16])
    for x in range(CX):
        down = pltpu.roll(low_end, (-(16 * x + 9)) % 128, 1)
        up = pltpu.roll(high_end, (127 - 16 * x) % 128, 1)
        add = jnp.where(lane8 < 2, down, jnp.where(lane8 == 127, up, 0.0))
        fm[pl.ds(8 * x, 8), :] = plane[x] + add
    after, before = flat.index((0, 1, 0)), flat.index((0, -1, 0))
    fm[pl.ds(7, 8, stride=8), :] += r0[before, 8:16]
    fm[pl.ds(0, 8, stride=8), :] += r0[after, 8:16]
    fm[pl.ds(1, 8, stride=8), :] += r0[after, 16:24]
    left = jnp.where(
        index8 < 8, low_end, jnp.where(index8 == 8, low_end + own_end, 0.0)
    )
    right = jnp.where((index8 == 1) | (index8 == 2), high_end + own_end, high_end)
    both_ends = jnp.concatenate([left, right], axis=0).astype(bf16)
    hb[0:16] = both_ends
    wrapped = jnp.where(lane8 < 64, pltpu.roll(right, 15, 1), pltpu.roll(left, 7, 1))
    hb[80:96] = jnp.concatenate([fm[pl.ds(56, 8), :], wrapped], axis=0).astype(bf16)
    for m in range(4):
        hb[16 + 16 * m : 32 + 16 * m] = fm[pl.ds(16 * m, 16), :].astype(bf16)

    halo = []
    for n, (dx, dy) in enumerate(HALO):
        start, rows = {2: (80, 16), -2: (0, 32)}.get(dx, (0, 80))
        copy = pltpu.make_async_remote_copy(
            src_ref=hb.at[pl.ds(start, rows)], dst_ref=rh.at[n, pl.ds(0, rows)],
            send_sem=send2.at[n], recv_sem=recv2.at[n],
            device_id=device_at(dx, dy, 0), device_id_type=MESH,
        )
        copy.start()
        halo.append(copy)

    xf[...] = jnp.zeros_like(xf)
    for i in range(SPAN):
        xf[32 * (i + 1) : 32 * (i + 1) + SPAN, 0:SPAN] = kern_ref[i].astype(f32)
    xb = xf[...].astype(bf16)
    eye = (
        lax.broadcasted_iota(jnp.int32, (24, 128), 0)
        == lax.broadcasted_iota(jnp.int32, (24, 128), 1)
    ).astype(f32).astype(bf16)
    blocks = []
    for h in range(2):
        kt = mm_nt(eye, xb[32 * (1 - h) : 32 * (1 - h) + 640])
        blocks += [kt[:, 128 * g : 128 * g + 128] for g in range(5)]
    lhs = jnp.concatenate(blocks, axis=0).astype(bf16)
    drow = lax.broadcasted_iota(jnp.int32, (128, 128), 0)
    dlane = lax.broadcasted_iota(jnp.int32, (128, 128), 1)
    base = (drow >> 6) * 64 + ((drow >> 5) & 1) * 8

    def shifted(n, carry):
        r = jnp.where(n < 10, n, 15)
        y = jnp.where(n < 10, n, -1)
        jy = ((drow & 31) + y) & 31
        target = base + (jy >> 3) * 16 + (jy & 7)
        sel = (dlane == target).astype(f32).astype(bf16)
        out = mm(lhs, sel)
        for h in range(2):
            for g in range(5):
                for c in range(3):
                    at = h * 120 + g * 24 + 8 * c
                    tf[g, pl.ds(h * 384 + 128 * c + r, 8, stride=16), :] = out[at : at + 8]
        return carry

    lax.fori_loop(0, 11, shifted, 0)
    for h in range(2):
        for g in range(5):
            for r in range(10, 15):
                for c in range(3):
                    tf[g, pl.ds(h * 384 + 128 * c + r, 8, stride=16), :] = jnp.zeros((8, 128), f32)
            tb[272 * h : 272 * h + 272, 128 * g : 128 * g + 128] = (
                tf[g, 384 * h : 384 * h + 272, :].astype(bf16)
            )

    def place(ends_bf16, main, xp, b, slots):
        at = xp * 64 + b * 16
        w[at : at + 16, 0:128] = main
        wide = ends_bf16.astype(f32)
        tops = []
        for s in slots:
            lo = pltpu.roll(wide[0:8], (119 - 16 * s) % 128, 1)
            hi = pltpu.roll(wide[8:16], (-1 - 16 * s) % 128, 1)
            tops.append(jnp.where(lane8 < 64, hi, lo))
        w[at : at + 16, 128:256] = jnp.concatenate(tops, axis=0).astype(bf16)

    for m in range(4):
        place(hb[0:16], hb[16 + 16 * m : 32 + 16 * m], 5 + m, 1, (2 * m, 2 * m + 1))
    def receive(n):
        dx, dy = HALO[n]
        halo[n].wait_recv()
        sx, b = -dx, (1 - dy) % 4
        if sx == 2:
            place(rh[n, 0:16], rh[n, 16:32], 13, b, (0, 1))
        elif sx == -2:
            last = rh[n, 0:16].astype(f32)
            blank = jnp.zeros((8, 128), f32)
            for half in range(2):
                w[16 * b : 16 * b + 16, 128 * half : 128 * half + 128] = jnp.concatenate(
                    [blank, last[8 * half : 8 * half + 8]], axis=0
                ).astype(bf16)
        else:
            for m in range(4):
                place(
                    rh[n, 0:16], rh[n, 16 + 16 * m : 32 + 16 * m],
                    4 * sx + 5 + m, b, (2 * m, 2 * m + 1),
                )

    def convolve(p):
        skip = 272 if p == 0 else 0
        out = mm(tb[skip:544, 0:576], w[64 * p : 64 * p + 576, :])
        for h in range(skip // 272, 2):
            acc = None
            for k in range(SPAN):
                at = 272 * h + 16 * k - skip
                term = out[at : at + 16]
                if k != 8:
                    term = pltpu.roll(term, (8 - k) % 256, 1)
                acc = term if acc is None else acc + term
            main, far = acc[:, 0:128], acc[:, 128:256]
            tail = jnp.where(
                (lane16 == 9) | (lane16 == 10),
                pltpu.roll(far, 9, 1),
                jnp.where(lane16 == 16, pltpu.roll(far, 17, 1), 0.0),
            )
            at = (2 * p + h) * 16
            mh, ml = split(main)
            th, tl = split(tail)
            phh[at : at + 16, 0:128] = mh
            phh[at : at + 16, 128:256] = th
            phl[at : at + 16, 0:128] = ml
            phl[at : at + 16, 128:256] = tl
            if 1 <= p <= 4:
                pot_ref[2 * p + h - 2] = main[0:8]

    upward = sum(1 for dx, _ in HALO if dx > 0)
    for n in reversed(range(upward, len(HALO))):
        receive(n)
    convolve(5)
    for n in reversed(range(upward)):
        receive(n)
    for p in range(5):
        convolve(p)

    for t in range(TILES):
        at = (t + 1) * 16
        high = phh[at : at + 64, 0:ZROWS]
        both = jnp.concatenate([high, phl[at : at + 64, 0:ZROWS]], axis=0)
        a = mm(both, zwh[t])
        value = a[:64] + a[64:] + mm(high, zwl[t])
        a = mm(both, zsh[t])
        slope = a[:64] + a[64:] + mm(high, zsl[t])
        fx = fy = fz = None
        for k in range(4):
            v, s = value[16 * k : 16 * k + 16], slope[16 * k : 16 * k + 16]
            wx, sx = xs[k, t : t + 1, :], xs[4 + k, t : t + 1, :]
            ax, ay, az = sx * v, wx * v, wx * s
            fx = ax if fx is None else fx + ax
            fy = ay if fy is None else fy + ay
            fz = az if fz is None else fz + az
        wy, sy = ys[0, t], ys[1, t]
        frc_ref[0, t, 0] = jnp.sum(fx * wy, axis=0, keepdims=True)
        frc_ref[1, t, 0] = -jnp.sum(fy * sy, axis=0, keepdims=True)
        frc_ref[2, t, 0] = -jnp.sum(fz * wy, axis=0, keepdims=True)

    for copy in fold:
        copy.wait_send()
    for copy in halo:
        copy.wait_send()


def local(charges, offsets, cells, kernel):
    f32, bf16 = jnp.float32, jnp.bfloat16
    vmem = pl.BlockSpec(memory_space=pltpu.VMEM)
    return pl.pallas_call(
        body,
        out_shape=(
            pltpu.VMEM((CX, CY, CZ), f32),
            pltpu.VMEM((3, TILES, 1, 1, APT), f32),
        ),
        in_specs=[pl.BlockSpec(memory_space=pltpu.HBM)] * 4,
        out_specs=(vmem, vmem),
        scratch_shapes=[
            pltpu.VMEM((TILES, APT), f32),
            pltpu.VMEM((3, TILES, APT), f32),
            pltpu.VMEM((2, TILES, APT), jnp.int32),
            pltpu.VMEM((SPAN, SPAN, SPAN), bf16),
            pltpu.VMEM((2, TILES, 16, APT), f32),
            pltpu.VMEM((8, TILES, APT), f32),
            pltpu.VMEM((ZROWS, 128), f32),
            pltpu.VMEM((TILES, ZROWS, APT), bf16),
            pltpu.VMEM((TILES, ZROWS, APT), bf16),
            pltpu.VMEM((TILES, ZROWS, APT), bf16),
            pltpu.VMEM((TILES, ZROWS, APT), bf16),
            pltpu.VMEM((16 * (CX + 3), 128), f32),
            pltpu.VMEM((16 * (CX + 3), 128), f32),
            pltpu.VMEM((2, 2, 2, 8, 128), f32),
            pltpu.VMEM((8, 24, 128), f32),
            pltpu.VMEM((len(FOLD), 8, 128), f32),
            pltpu.VMEM((8, 24, 128), f32),
            pltpu.VMEM((72, 128), f32),
            pltpu.VMEM((96, 128), bf16),
            pltpu.VMEM((len(HALO), 80, 128), bf16),
            pltpu.VMEM((32 * 21, 128), f32),
            pltpu.VMEM((5, 784, 128), f32),
            pltpu.VMEM((544, 640), bf16),
            pltpu.VMEM((14 * 64, 256), bf16),
            pltpu.VMEM((192, 256), bf16),
            pltpu.VMEM((192, 256), bf16),
            pltpu.SemaphoreType.DMA((4,)),
            pltpu.SemaphoreType.DMA((len(FOLD),)),
            pltpu.SemaphoreType.DMA((len(FOLD),)),
            pltpu.SemaphoreType.DMA((len(HALO),)),
            pltpu.SemaphoreType.DMA((len(HALO),)),
        ],
        compiler_params=pltpu.CompilerParams(
            collective_id=0, has_side_effects=True, vmem_limit_bytes=60 * 1024 * 1024
        ),
    )(charges, offsets, cells, kernel)


def solution(mesh):
    placed = (
        P("gx", "gy", "gz", None),
        P(None, "gx", "gy", "gz", None),
        P(None, "gx", "gy", "gz", None),
        P(),
    )
    return jax.shard_map(
        local,
        mesh=mesh,
        in_specs=placed,
        out_specs=(P("gx", "gy", "gz"), P(None, "gx", "gy", "gz", None)),
        check_vma=False,
    )
```

```python
import jax
import jax.numpy as jnp
from jax import lax
from jax.experimental import pallas as pl
from jax.experimental.pallas import tpu as pltpu
from jax.sharding import PartitionSpec as P

CX = 8
CY = 8
CZ = 128
TILES = 8
APT = 512
SPAN = 17
ZROWS = 160
MESH = pl.DeviceIdType.MESH

FOLD = [
    (dx, dy, dz)
    for dx in (1, 0, -1)
    for dy, dz in ((1, 1), (-1, 1), (1, -1), (-1, -1), (0, 1), (0, -1), (1, 0), (-1, 0), (0, 0))
    if (dx, dy, dz) != (0, 0, 0)
]
HALO = [(dx, dy) for dy in (2, 1, -1, 0) for dx in (2, 1)]
HALO += [(0, dy) for dy in (2, 1, -1)]
HALO += [(dx, dy) for dy in (2, 1, -1, 0) for dx in (-2, -1)]
PEERS = FOLD


def neighbours():
    tables = []
    for axis in ("gx", "gy", "gz"):
        size = lax.axis_size(axis)
        index = lax.axis_index(axis)
        table = {0: index}
        for step in (1, 2):
            up, down = index + step, index - step
            table[step] = jnp.where(up >= size, up - size, up)
            table[-step] = jnp.where(down < 0, down + size, down)
        table[3] = table[-1]
        tables.append(table)
    return lambda dx, dy, dz: (tables[0][dx], tables[1][dy], tables[2][dz])


def x_splines(f):
    r = 1.0 - f
    values = [
        r * r * r / 6.0,
        (3.0 * f * f * f - 6.0 * f * f + 4.0) / 6.0,
        (-3.0 * f * f * f + 3.0 * f * f + 3.0 * f + 1.0) / 6.0,
        f * f * f / 6.0,
    ]
    slopes = [-0.5 * r * r, 1.5 * f * f - 2.0 * f, -1.5 * f * f + f + 0.5, 0.5 * f * f]
    return values, slopes


def bspline(u):
    a = jnp.abs(u)
    p = jnp.maximum(2.0 - a, 0.0)
    q = jnp.maximum(1.0 - a, 0.0)
    return p * p * p * (1.0 / 6.0) - q * q * q * (2.0 / 3.0)


def bslope(u):
    a = jnp.abs(u)
    p = jnp.maximum(2.0 - a, 0.0)
    q = jnp.maximum(1.0 - a, 0.0)
    m = 0.5 * p * p - 2.0 * q * q
    return jnp.where(u < 0.0, -m, m)


def split(value):
    high = value.astype(jnp.bfloat16)
    low = (value - high.astype(jnp.float32)).astype(jnp.bfloat16)
    return high, low


def mm(a, b):
    return jnp.dot(a, b, preferred_element_type=jnp.float32)


def mm_nt(a, b):
    return lax.dot_general(a, b, (((1,), (1,)), ((), ())), preferred_element_type=jnp.float32)


def body(
    q_hbm, off_hbm, cell_hbm, kern_hbm, pot_ref, frc_ref,
    q_ref, off_ref, cell_ref, kern_ref, ys, xs,
    zrow, zwh, zwl, zsh, zsl, pm, pe, zbuf, sbuf, rz, r0, fm, hb, rh,
    xf, tf, tb, w, phh, phl, load, send1, recv1, send2, recv2,
):
    iy = lax.axis_index("gy")
    iz = lax.axis_index("gz")
    f32, bf16 = jnp.float32, jnp.bfloat16

    device_at = neighbours()
    barrier = pltpu.get_barrier_semaphore()
    for peer in PEERS:
        pl.semaphore_signal(barrier, inc=1, device_id=device_at(*peer), device_id_type=MESH)

    loads = [
        pltpu.make_async_copy(q_hbm.at[:, 0, 0, :], q_ref, load.at[0]),
        pltpu.make_async_copy(off_hbm.at[:, :, 0, 0, :], off_ref, load.at[1]),
        pltpu.make_async_copy(cell_hbm.at[:, :, 0, 0, :], cell_ref, load.at[2]),
        pltpu.make_async_copy(kern_hbm, kern_ref, load.at[3]),
    ]
    for copy in loads:
        copy.start()

    row_id = lax.broadcasted_iota(jnp.int32, (ZROWS, 128), 0)
    zrow[...] = jnp.where(
        row_id < 128, row_id, jnp.where(row_id < 144, row_id - 9, row_id - 145)
    ).astype(f32)
    pm[...] = jnp.zeros_like(pm)
    pe[...] = jnp.zeros_like(pe)
    y_id = lax.broadcasted_iota(jnp.int32, (16, APT), 0)
    y_id = jnp.where(y_id < 15, y_id, -1).astype(f32)

    def y_distance(t):
        ly = (cell_ref[0, pl.ds(t, 1), :] - iy * CY).astype(f32)
        return (y_id - ly) - off_ref[1, pl.ds(t, 1), :]

    def z_position(t):
        return (cell_ref[1, pl.ds(t, 1), :] - iz * CZ).astype(f32) + off_ref[2, pl.ds(t, 1), :]

    for copy in loads:
        copy.wait()
    values, derivatives = x_splines(off_ref[0])
    for k in range(4):
        xs[k] = q_ref[...] * values[k]
        xs[4 + k] = -q_ref[...] * derivatives[k]

    def spread(t, carry):
        zpos = z_position(t)
        for c in range(ZROWS // 16):
            zz = zrow[pl.ds(16 * c, 16), :]
            u = jnp.concatenate([zz] * 4, axis=1) - zpos
            high, low = split(bspline(u))
            zwh[t, pl.ds(16 * c, 16), :] = high
            zwl[t, pl.ds(16 * c, 16), :] = low
        wy = bspline(y_distance(t))
        ys[0, t] = wy
        parts = [split(xs[k, pl.ds(t, 1), :] * wy) for k in range(4)]
        high = jnp.concatenate([p[0] for p in parts], axis=0)
        both = jnp.concatenate([high] + [p[1] for p in parts], axis=0)
        first = mm_nt(both, zwh[t])
        total = first[:64] + first[64:] + mm_nt(high, zwl[t])
        for k in range(4):
            at = pl.multiple_of((t + k) * 16, 16)
            pm[pl.ds(at, 16), :] += total[16 * k : 16 * k + 16, :128]
            pe[pl.ds(at, 16), 0:32] += total[16 * k : 16 * k + 16, 128:160]
        return carry

    lax.fori_loop(0, TILES, spread, 0, unroll=2)

    lane16 = lax.broadcasted_iota(jnp.int32, (16, 128), 1)
    index16 = lane16 & 15
    zero16 = jnp.zeros((16, 128), f32)
    zr = [zero16, zero16]
    zl = [zero16, zero16]
    for n in range(CX + 3):
        x = n - 1
        part, slot = (0, x) if 0 <= x < 8 else (1, x % 8)
        e = pe[pl.ds(16 * n, 16), :]
        er = jnp.where(lane16 < 16, e, 0.0)
        el = jnp.where((lane16 >= 16) & (lane16 < 32), e, 0.0)
        zr[part] = zr[part] + pltpu.roll(er, 16 * slot, 1)
        zl[part] = zl[part] + pltpu.roll(el, (16 * slot + 112) % 128, 1)
    ends = []
    for part in range(2):
        ends.append(
            jnp.where(
                (index16 == 1) | (index16 == 2),
                pltpu.roll(zr[part], 120, 1),
                jnp.where(index16 == 8, pltpu.roll(zl[part], 8, 1), 0.0),
            )
        )
        for half in range(2):
            zbuf[0, half, part] = zr[part][8 * half : 8 * half + 8]
            zbuf[1, half, part] = zl[part][8 * half : 8 * half + 8]
    row8 = lax.broadcasted_iota(jnp.int32, (8, 128), 0)
    flat = [m for m in FOLD if m[2] == 0]
    for n, (dx, dy, _) in enumerate(flat):
        half, part = int(dy != 0), int(dx != 0)
        if dx and dy:
            tile = ends[part][8:16]
            planes = (0,) if dx < 0 else (9, 10)
            for m in reversed(range(len(planes) + 1)):
                if m < len(planes):
                    part_m = pm[pl.ds(16 * planes[m] + 8, 8), :]
                else:
                    part_m = ends[part][8:16]
                moved = pltpu.roll(part_m, 2 * m if dy > 0 else m, 0) if m else part_m
                if dy > 0:
                    here = (row8 >> 1) == m
                else:
                    here = row8 == (7 + m) % 8
                tile = jnp.where(here, moved, tile)
            sbuf[n, 0:8] = tile
            continue
        sbuf[n, 0:8] = ends[part][8 * half : 8 * half + 8]
        if dx == 0:
            rows = (15,) if dy < 0 else (8, 9)
            for m, r in enumerate(rows):
                sbuf[n, 8 + 8 * m : 16 + 8 * m] = pm[pl.ds(16 + r, 8, stride=16), :]
        else:
            planes = (0,) if dx < 0 else (9, 10)
            for m, r in enumerate(planes):
                sbuf[n, 8 + 8 * m : 16 + 8 * m] = pm[pl.ds(16 * r + 8 * half, 8), :]

    pl.semaphore_wait(barrier, len(PEERS))

    fold = []
    for n, (dx, dy, dz) in enumerate(FOLD):
        if dz:
            side = 0 if dz > 0 else 1
            src = zbuf.at[side, int(dy != 0), int(dx != 0)]
            dst = rz.at[n]
        else:
            m = flat.index((dx, dy, dz))
            rows = 8 if dx and dy else 16 if dx < 0 or dy < 0 else 24
            src = sbuf.at[m, pl.ds(0, rows)]
            dst = r0.at[m, pl.ds(0, rows)]
        copy = pltpu.make_async_remote_copy(
            src_ref=src, dst_ref=dst, send_sem=send1.at[n], recv_sem=recv1.at[n],
            device_id=device_at(dx, dy, dz), device_id_type=MESH,
        )
        copy.start()
        fold.append(copy)

    def slopes(t, carry):
        zpos = z_position(t)
        ys[1, t] = bslope(y_distance(t))
        for c in range(ZROWS // 16):
            zz = zrow[pl.ds(16 * c, 16), :]
            u = jnp.concatenate([zz] * 4, axis=1) - zpos
            high, low = split(bslope(u))
            zsh[t, pl.ds(16 * c, 16), :] = high
            zsl[t, pl.ds(16 * c, 16), :] = low
        return carry

    lax.fori_loop(0, TILES, slopes, 0)

    for copy in fold:
        copy.wait_recv()

    lane8 = lax.broadcasted_iota(jnp.int32, (8, 128), 1)
    slot8 = lane8 // 16
    index8 = lane8 & 15

    def rows_of(dy, value):
        if dy == 0:
            return value
        return jnp.where((row8 < 2) if dy > 0 else (row8 == 7), value, 0.0)

    def slots_of(dx, value):
        if dx == 0:
            return value
        return jnp.where((slot8 < 2) if dx > 0 else (slot8 == 7), value, 0.0)

    low_end = jnp.zeros((8, 128), f32)
    high_end = jnp.zeros((8, 128), f32)
    own_end = ends[0][0:8]
    plane = [pm[pl.ds(16 * (x + 1), 8), :] for x in range(CX)]
    for n, (dx, dy, dz) in enumerate(FOLD):
        if dz > 0:
            low_end = low_end + slots_of(dx, rows_of(dy, rz[n]))
        elif dz < 0:
            high_end = high_end + slots_of(dx, rows_of(dy, rz[n]))
        else:
            m = flat.index((dx, dy, dz))
            if dx and dy:
                step = 2 if dy > 0 else 1
                count = 3 if dx > 0 else 2
                got = [r0[m, 0:8]] + [pltpu.roll(r0[m, 0:8], 8 - step * j, 0) for j in range(1, count)]
                got = [rows_of(dy, value) for value in got]
                own_end = own_end + slots_of(dx, got[-1])
                for x, value in zip((0, 1) if dx > 0 else (7,), got):
                    plane[x] = plane[x] + value
                continue
            own_end = own_end + slots_of(dx, rows_of(dy, r0[m, 0:8]))
            if dx > 0:
                plane[0] = plane[0] + rows_of(dy, r0[m, 8:16])
                plane[1] = plane[1] + rows_of(dy, r0[m, 16:24])
            elif dx < 0:
                plane[7] = plane[7] + rows_of(dy, r0[m, 8:16])
    for x in range(CX):
        down = pltpu.roll(low_end, (-(16 * x + 9)) % 128, 1)
        up = pltpu.roll(high_end, (127 - 16 * x) % 128, 1)
        add = jnp.where(lane8 < 2, down, jnp.where(lane8 == 127, up, 0.0))
        fm[pl.ds(8 * x, 8), :] = plane[x] + add
    after, before = flat.index((0, 1, 0)), flat.index((0, -1, 0))
    fm[pl.ds(7, 8, stride=8), :] += r0[before, 8:16]
    fm[pl.ds(0, 8, stride=8), :] += r0[after, 8:16]
    fm[pl.ds(1, 8, stride=8), :] += r0[after, 16:24]
    left = jnp.where(
        index8 < 8, low_end, jnp.where(index8 == 8, low_end + own_end, 0.0)
    )
    right = jnp.where((index8 == 1) | (index8 == 2), high_end + own_end, high_end)
    both_ends = jnp.concatenate([left, right], axis=0).astype(bf16)
    hb[0:16] = both_ends
    wrapped = jnp.where(lane8 < 64, pltpu.roll(right, 15, 1), pltpu.roll(left, 7, 1))
    hb[80:96] = jnp.concatenate([fm[pl.ds(56, 8), :], wrapped], axis=0).astype(bf16)
    for m in range(4):
        hb[16 + 16 * m : 32 + 16 * m] = fm[pl.ds(16 * m, 16), :].astype(bf16)

    halo = []
    for n, (dx, dy) in enumerate(HALO):
        start, rows = {2: (80, 16), -2: (0, 32)}.get(dx, (0, 80))
        copy = pltpu.make_async_remote_copy(
            src_ref=hb.at[pl.ds(start, rows)], dst_ref=rh.at[n, pl.ds(0, rows)],
            send_sem=send2.at[n], recv_sem=recv2.at[n],
            device_id=device_at(dx, dy, 0), device_id_type=MESH,
        )
        copy.start()
        halo.append(copy)

    xf[...] = jnp.zeros_like(xf)
    for i in range(SPAN):
        xf[32 * (i + 1) : 32 * (i + 1) + SPAN, 0:SPAN] = kern_ref[i].astype(f32)
    xb = xf[...].astype(bf16)
    eye = (
        lax.broadcasted_iota(jnp.int32, (24, 128), 0)
        == lax.broadcasted_iota(jnp.int32, (24, 128), 1)
    ).astype(f32).astype(bf16)
    blocks = []
    for h in range(2):
        kt = mm_nt(eye, xb[32 * (1 - h) : 32 * (1 - h) + 640])
        blocks += [kt[:, 128 * g : 128 * g + 128] for g in range(5)]
    lhs = jnp.concatenate(blocks, axis=0).astype(bf16)
    drow = lax.broadcasted_iota(jnp.int32, (128, 128), 0)
    dlane = lax.broadcasted_iota(jnp.int32, (128, 128), 1)
    base = (drow >> 6) * 64 + ((drow >> 5) & 1) * 8

    def shifted(n, carry):
        r = jnp.where(n < 10, n, 15)
        y = jnp.where(n < 10, n, -1)
        jy = ((drow & 31) + y) & 31
        target = base + (jy >> 3) * 16 + (jy & 7)
        sel = (dlane == target).astype(f32).astype(bf16)
        out = mm(lhs, sel)
        for h in range(2):
            for g in range(5):
                for c in range(3):
                    at = h * 120 + g * 24 + 8 * c
                    tf[g, pl.ds(h * 384 + 128 * c + r, 8, stride=16), :] = out[at : at + 8]
        return carry

    lax.fori_loop(0, 11, shifted, 0)
    for h in range(2):
        for g in range(5):
            for r in range(10, 15):
                for c in range(3):
                    tf[g, pl.ds(h * 384 + 128 * c + r, 8, stride=16), :] = jnp.zeros((8, 128), f32)
            tb[272 * h : 272 * h + 272, 128 * g : 128 * g + 128] = (
                tf[g, 384 * h : 384 * h + 272, :].astype(bf16)
            )

    def place(ends_bf16, main, xp, b, slots):
        at = xp * 64 + b * 16
        w[at : at + 16, 0:128] = main
        wide = ends_bf16.astype(f32)
        tops = []
        for s in slots:
            lo = pltpu.roll(wide[0:8], (119 - 16 * s) % 128, 1)
            hi = pltpu.roll(wide[8:16], (-1 - 16 * s) % 128, 1)
            tops.append(jnp.where(lane8 < 64, hi, lo))
        w[at : at + 16, 128:256] = jnp.concatenate(tops, axis=0).astype(bf16)

    for m in range(4):
        place(hb[0:16], hb[16 + 16 * m : 32 + 16 * m], 5 + m, 1, (2 * m, 2 * m + 1))
    for n in reversed(range(len(HALO))):
        dx, dy = HALO[n]
        halo[n].wait_recv()
        sx, b = -dx, (1 - dy) % 4
        if sx == 2:
            place(rh[n, 0:16], rh[n, 16:32], 13, b, (0, 1))
        elif sx == -2:
            last = rh[n, 0:16].astype(f32)
            blank = jnp.zeros((8, 128), f32)
            for half in range(2):
                w[16 * b : 16 * b + 16, 128 * half : 128 * half + 128] = jnp.concatenate(
                    [blank, last[8 * half : 8 * half + 8]], axis=0
                ).astype(bf16)
        else:
            for m in range(4):
                place(
                    rh[n, 0:16], rh[n, 16 + 16 * m : 32 + 16 * m],
                    4 * sx + 5 + m, b, (2 * m, 2 * m + 1),
                )

    for p in range(6):
        skip = 272 if p == 0 else 0
        out = mm(tb[skip:544, 0:576], w[64 * p : 64 * p + 576, :])
        for h in range(skip // 272, 2):
            acc = None
            for k in range(SPAN):
                at = 272 * h + 16 * k - skip
                term = out[at : at + 16]
                if k != 8:
                    term = pltpu.roll(term, (8 - k) % 256, 1)
                acc = term if acc is None else acc + term
            main, far = acc[:, 0:128], acc[:, 128:256]
            tail = jnp.where(
                (lane16 == 9) | (lane16 == 10),
                pltpu.roll(far, 9, 1),
                jnp.where(lane16 == 16, pltpu.roll(far, 17, 1), 0.0),
            )
            at = (2 * p + h) * 16
            mh, ml = split(main)
            th, tl = split(tail)
            phh[at : at + 16, 0:128] = mh
            phh[at : at + 16, 128:256] = th
            phl[at : at + 16, 0:128] = ml
            phl[at : at + 16, 128:256] = tl
            if 1 <= p <= 4:
                pot_ref[2 * p + h - 2] = main[0:8]

    for t in range(TILES):
        at = (t + 1) * 16
        high = phh[at : at + 64, 0:ZROWS]
        both = jnp.concatenate([high, phl[at : at + 64, 0:ZROWS]], axis=0)
        a = mm(both, zwh[t])
        value = a[:64] + a[64:] + mm(high, zwl[t])
        a = mm(both, zsh[t])
        slope = a[:64] + a[64:] + mm(high, zsl[t])
        fx = fy = fz = None
        for k in range(4):
            v, s = value[16 * k : 16 * k + 16], slope[16 * k : 16 * k + 16]
            wx, sx = xs[k, t : t + 1, :], xs[4 + k, t : t + 1, :]
            ax, ay, az = sx * v, wx * v, wx * s
            fx = ax if fx is None else fx + ax
            fy = ay if fy is None else fy + ay
            fz = az if fz is None else fz + az
        wy, sy = ys[0, t], ys[1, t]
        frc_ref[0, t, 0] = jnp.sum(fx * wy, axis=0, keepdims=True)
        frc_ref[1, t, 0] = -jnp.sum(fy * sy, axis=0, keepdims=True)
        frc_ref[2, t, 0] = -jnp.sum(fz * wy, axis=0, keepdims=True)

    for copy in fold:
        copy.wait_send()
    for copy in halo:
        copy.wait_send()


def local(charges, offsets, cells, kernel):
    f32, bf16 = jnp.float32, jnp.bfloat16
    vmem = pl.BlockSpec(memory_space=pltpu.VMEM)
    return pl.pallas_call(
        body,
        out_shape=(
            pltpu.VMEM((CX, CY, CZ), f32),
            pltpu.VMEM((3, TILES, 1, 1, APT), f32),
        ),
        in_specs=[pl.BlockSpec(memory_space=pltpu.HBM)] * 4,
        out_specs=(vmem, vmem),
        scratch_shapes=[
            pltpu.VMEM((TILES, APT), f32),
            pltpu.VMEM((3, TILES, APT), f32),
            pltpu.VMEM((2, TILES, APT), jnp.int32),
            pltpu.VMEM((SPAN, SPAN, SPAN), bf16),
            pltpu.VMEM((2, TILES, 16, APT), f32),
            pltpu.VMEM((8, TILES, APT), f32),
            pltpu.VMEM((ZROWS, 128), f32),
            pltpu.VMEM((TILES, ZROWS, APT), bf16),
            pltpu.VMEM((TILES, ZROWS, APT), bf16),
            pltpu.VMEM((TILES, ZROWS, APT), bf16),
            pltpu.VMEM((TILES, ZROWS, APT), bf16),
            pltpu.VMEM((16 * (CX + 3), 128), f32),
            pltpu.VMEM((16 * (CX + 3), 128), f32),
            pltpu.VMEM((2, 2, 2, 8, 128), f32),
            pltpu.VMEM((8, 24, 128), f32),
            pltpu.VMEM((len(FOLD), 8, 128), f32),
            pltpu.VMEM((8, 24, 128), f32),
            pltpu.VMEM((72, 128), f32),
            pltpu.VMEM((96, 128), bf16),
            pltpu.VMEM((len(HALO), 80, 128), bf16),
            pltpu.VMEM((32 * 21, 128), f32),
            pltpu.VMEM((5, 784, 128), f32),
            pltpu.VMEM((544, 640), bf16),
            pltpu.VMEM((14 * 64, 256), bf16),
            pltpu.VMEM((192, 256), bf16),
            pltpu.VMEM((192, 256), bf16),
            pltpu.SemaphoreType.DMA((4,)),
            pltpu.SemaphoreType.DMA((len(FOLD),)),
            pltpu.SemaphoreType.DMA((len(FOLD),)),
            pltpu.SemaphoreType.DMA((len(HALO),)),
            pltpu.SemaphoreType.DMA((len(HALO),)),
        ],
        compiler_params=pltpu.CompilerParams(
            collective_id=0, has_side_effects=True, vmem_limit_bytes=60 * 1024 * 1024
        ),
    )(charges, offsets, cells, kernel)


def solution(mesh):
    placed = (
        P("gx", "gy", "gz", None),
        P(None, "gx", "gy", "gz", None),
        P(None, "gx", "gy", "gz", None),
        P(),
    )
    return jax.shard_map(
        local,
        mesh=mesh,
        in_specs=placed,
        out_specs=(P("gx", "gy", "gz"), P(None, "gx", "gy", "gz", None)),
        check_vma=False,
    )
```

```python
import jax
import jax.numpy as jnp
from jax import lax
from jax.experimental import pallas as pl
from jax.experimental.pallas import tpu as pltpu
from jax.sharding import PartitionSpec as P

CX = 8
CY = 8
CZ = 128
TILES = 8
APT = 512
SPAN = 17
ZROWS = 160
MESH = pl.DeviceIdType.MESH

FOLD = [
    (dx, dy, dz)
    for dx in (1, 0, -1)
    for dy, dz in ((1, 1), (-1, 1), (1, -1), (-1, -1), (0, 1), (0, -1), (1, 0), (-1, 0), (0, 0))
    if (dx, dy, dz) != (0, 0, 0)
]
HALO = [(dx, dy) for dy in (2, 1, -1, 0) for dx in (2, 1)]
HALO += [(0, dy) for dy in (2, 1, -1)]
HALO += [(dx, dy) for dy in (2, 1, -1, 0) for dx in (-2, -1)]
PEERS = FOLD


def neighbours():
    tables = []
    for axis in ("gx", "gy", "gz"):
        size = lax.axis_size(axis)
        index = lax.axis_index(axis)
        table = {0: index}
        for step in (1, 2):
            up, down = index + step, index - step
            table[step] = jnp.where(up >= size, up - size, up)
            table[-step] = jnp.where(down < 0, down + size, down)
        table[3] = table[-1]
        tables.append(table)
    return lambda dx, dy, dz: (tables[0][dx], tables[1][dy], tables[2][dz])


def x_splines(f):
    r = 1.0 - f
    values = [
        r * r * r / 6.0,
        (3.0 * f * f * f - 6.0 * f * f + 4.0) / 6.0,
        (-3.0 * f * f * f + 3.0 * f * f + 3.0 * f + 1.0) / 6.0,
        f * f * f / 6.0,
    ]
    slopes = [-0.5 * r * r, 1.5 * f * f - 2.0 * f, -1.5 * f * f + f + 0.5, 0.5 * f * f]
    return values, slopes


def bspline(u):
    a = jnp.abs(u)
    p = jnp.maximum(2.0 - a, 0.0)
    q = jnp.maximum(1.0 - a, 0.0)
    return p * p * p * (1.0 / 6.0) - q * q * q * (2.0 / 3.0)


def bslope(u):
    a = jnp.abs(u)
    p = jnp.maximum(2.0 - a, 0.0)
    q = jnp.maximum(1.0 - a, 0.0)
    m = 0.5 * p * p - 2.0 * q * q
    return jnp.where(u < 0.0, -m, m)


def split(value):
    high = value.astype(jnp.bfloat16)
    low = (value - high.astype(jnp.float32)).astype(jnp.bfloat16)
    return high, low


def mm(a, b):
    return jnp.dot(a, b, preferred_element_type=jnp.float32)


def mm_nt(a, b):
    return lax.dot_general(a, b, (((1,), (1,)), ((), ())), preferred_element_type=jnp.float32)


def body(
    q_hbm, off_hbm, cell_hbm, kern_hbm, pot_ref, frc_ref,
    q_ref, off_ref, cell_ref, kern_ref, ys, xs,
    zrow, zwh, zwl, zsh, zsl, pm, pe, zbuf, sbuf, rz, r0, fm, hb, rh,
    xf, tf, tb, w, phh, phl, load, send1, recv1, send2, recv2,
):
    iy = lax.axis_index("gy")
    iz = lax.axis_index("gz")
    f32, bf16 = jnp.float32, jnp.bfloat16

    device_at = neighbours()
    barrier = pltpu.get_barrier_semaphore()
    for peer in PEERS:
        pl.semaphore_signal(barrier, inc=1, device_id=device_at(*peer), device_id_type=MESH)

    loads = [
        pltpu.make_async_copy(q_hbm.at[:, 0, 0, :], q_ref, load.at[0]),
        pltpu.make_async_copy(off_hbm.at[:, :, 0, 0, :], off_ref, load.at[1]),
        pltpu.make_async_copy(cell_hbm.at[:, :, 0, 0, :], cell_ref, load.at[2]),
        pltpu.make_async_copy(kern_hbm, kern_ref, load.at[3]),
    ]
    for copy in loads:
        copy.start()

    row_id = lax.broadcasted_iota(jnp.int32, (ZROWS, 128), 0)
    zrow[...] = jnp.where(
        row_id < 128, row_id, jnp.where(row_id < 144, row_id - 9, row_id - 145)
    ).astype(f32)
    pm[...] = jnp.zeros_like(pm)
    pe[...] = jnp.zeros_like(pe)
    y_id = lax.broadcasted_iota(jnp.int32, (16, APT), 0)
    y_id = jnp.where(y_id < 15, y_id, -1).astype(f32)

    def y_distance(t):
        ly = (cell_ref[0, pl.ds(t, 1), :] - iy * CY).astype(f32)
        return (y_id - ly) - off_ref[1, pl.ds(t, 1), :]

    def z_position(t):
        return (cell_ref[1, pl.ds(t, 1), :] - iz * CZ).astype(f32) + off_ref[2, pl.ds(t, 1), :]

    for copy in loads:
        copy.wait()
    values, derivatives = x_splines(off_ref[0])
    for k in range(4):
        xs[k] = q_ref[...] * values[k]
        xs[4 + k] = -q_ref[...] * derivatives[k]

    def spread(t, carry):
        zpos = z_position(t)
        for c in range(ZROWS // 16):
            zz = zrow[pl.ds(16 * c, 16), :]
            u = jnp.concatenate([zz] * 4, axis=1) - zpos
            high, low = split(bspline(u))
            zwh[t, pl.ds(16 * c, 16), :] = high
            zwl[t, pl.ds(16 * c, 16), :] = low
        wy = bspline(y_distance(t))
        ys[0, t] = wy
        parts = [split(xs[k, pl.ds(t, 1), :] * wy) for k in range(4)]
        high = jnp.concatenate([p[0] for p in parts], axis=0)
        both = jnp.concatenate([high] + [p[1] for p in parts], axis=0)
        first = mm_nt(both, zwh[t])
        total = first[:64] + first[64:] + mm_nt(high, zwl[t])
        for k in range(4):
            at = pl.multiple_of((t + k) * 16, 16)
            pm[pl.ds(at, 16), :] += total[16 * k : 16 * k + 16, :128]
            pe[pl.ds(at, 16), 0:32] += total[16 * k : 16 * k + 16, 128:160]
        return carry

    lax.fori_loop(0, TILES, spread, 0, unroll=2)

    lane16 = lax.broadcasted_iota(jnp.int32, (16, 128), 1)
    index16 = lane16 & 15
    zero16 = jnp.zeros((16, 128), f32)
    zr = [zero16, zero16]
    zl = [zero16, zero16]
    for n in range(CX + 3):
        x = n - 1
        part, slot = (0, x) if 0 <= x < 8 else (1, x % 8)
        e = pe[pl.ds(16 * n, 16), :]
        er = jnp.where(lane16 < 16, e, 0.0)
        el = jnp.where((lane16 >= 16) & (lane16 < 32), e, 0.0)
        zr[part] = zr[part] + pltpu.roll(er, 16 * slot, 1)
        zl[part] = zl[part] + pltpu.roll(el, (16 * slot + 112) % 128, 1)
    ends = []
    for part in range(2):
        ends.append(
            jnp.where(
                (index16 == 1) | (index16 == 2),
                pltpu.roll(zr[part], 120, 1),
                jnp.where(index16 == 8, pltpu.roll(zl[part], 8, 1), 0.0),
            )
        )
        for half in range(2):
            zbuf[0, half, part] = zr[part][8 * half : 8 * half + 8]
            zbuf[1, half, part] = zl[part][8 * half : 8 * half + 8]
    row8 = lax.broadcasted_iota(jnp.int32, (8, 128), 0)
    flat = [m for m in FOLD if m[2] == 0]
    for n, (dx, dy, _) in enumerate(flat):
        half, part = int(dy != 0), int(dx != 0)
        if dx and dy:
            tile = ends[part][8:16]
            planes = (0,) if dx < 0 else (9, 10)
            for m in reversed(range(len(planes) + 1)):
                if m < len(planes):
                    part_m = pm[pl.ds(16 * planes[m] + 8, 8), :]
                else:
                    part_m = ends[part][8:16]
                moved = pltpu.roll(part_m, 2 * m if dy > 0 else m, 0) if m else part_m
                if dy > 0:
                    here = (row8 >> 1) == m
                else:
                    here = row8 == (7 + m) % 8
                tile = jnp.where(here, moved, tile)
            sbuf[n, 0:8] = tile
            continue
        sbuf[n, 0:8] = ends[part][8 * half : 8 * half + 8]
        if dx == 0:
            rows = (15,) if dy < 0 else (8, 9)
            for m, r in enumerate(rows):
                sbuf[n, 8 + 8 * m : 16 + 8 * m] = pm[pl.ds(16 + r, 8, stride=16), :]
        else:
            planes = (0,) if dx < 0 else (9, 10)
            for m, r in enumerate(planes):
                sbuf[n, 8 + 8 * m : 16 + 8 * m] = pm[pl.ds(16 * r + 8 * half, 8), :]

    pl.semaphore_wait(barrier, len(PEERS))

    fold = []
    for n, (dx, dy, dz) in enumerate(FOLD):
        if dz:
            side = 0 if dz > 0 else 1
            src = zbuf.at[side, int(dy != 0), int(dx != 0)]
            dst = rz.at[n]
        else:
            m = flat.index((dx, dy, dz))
            rows = 8 if dx and dy else 16 if dx < 0 or dy < 0 else 24
            src = sbuf.at[m, pl.ds(0, rows)]
            dst = r0.at[m, pl.ds(0, rows)]
        copy = pltpu.make_async_remote_copy(
            src_ref=src, dst_ref=dst, send_sem=send1.at[n], recv_sem=recv1.at[n],
            device_id=device_at(dx, dy, dz), device_id_type=MESH,
        )
        copy.start()
        fold.append(copy)

    def slopes(t, carry):
        zpos = z_position(t)
        ys[1, t] = bslope(y_distance(t))
        for c in range(ZROWS // 16):
            zz = zrow[pl.ds(16 * c, 16), :]
            u = jnp.concatenate([zz] * 4, axis=1) - zpos
            high, low = split(bslope(u))
            zsh[t, pl.ds(16 * c, 16), :] = high
            zsl[t, pl.ds(16 * c, 16), :] = low
        return carry

    lax.fori_loop(0, TILES, slopes, 0)

    for copy in fold:
        copy.wait_recv()

    lane8 = lax.broadcasted_iota(jnp.int32, (8, 128), 1)
    slot8 = lane8 // 16
    index8 = lane8 & 15

    def rows_of(dy, value):
        if dy == 0:
            return value
        return jnp.where((row8 < 2) if dy > 0 else (row8 == 7), value, 0.0)

    def slots_of(dx, value):
        if dx == 0:
            return value
        return jnp.where((slot8 < 2) if dx > 0 else (slot8 == 7), value, 0.0)

    low_end = jnp.zeros((8, 128), f32)
    high_end = jnp.zeros((8, 128), f32)
    own_end = ends[0][0:8]
    plane = [pm[pl.ds(16 * (x + 1), 8), :] for x in range(CX)]
    for n, (dx, dy, dz) in enumerate(FOLD):
        if dz > 0:
            low_end = low_end + slots_of(dx, rows_of(dy, rz[n]))
        elif dz < 0:
            high_end = high_end + slots_of(dx, rows_of(dy, rz[n]))
        else:
            m = flat.index((dx, dy, dz))
            if dx and dy:
                step = 2 if dy > 0 else 1
                count = 3 if dx > 0 else 2
                got = [r0[m, 0:8]] + [pltpu.roll(r0[m, 0:8], 8 - step * j, 0) for j in range(1, count)]
                got = [rows_of(dy, value) for value in got]
                own_end = own_end + slots_of(dx, got[-1])
                for x, value in zip((0, 1) if dx > 0 else (7,), got):
                    plane[x] = plane[x] + value
                continue
            own_end = own_end + slots_of(dx, rows_of(dy, r0[m, 0:8]))
            if dx > 0:
                plane[0] = plane[0] + rows_of(dy, r0[m, 8:16])
                plane[1] = plane[1] + rows_of(dy, r0[m, 16:24])
            elif dx < 0:
                plane[7] = plane[7] + rows_of(dy, r0[m, 8:16])
    for x in range(CX):
        down = pltpu.roll(low_end, (-(16 * x + 9)) % 128, 1)
        up = pltpu.roll(high_end, (127 - 16 * x) % 128, 1)
        add = jnp.where(lane8 < 2, down, jnp.where(lane8 == 127, up, 0.0))
        fm[pl.ds(8 * x, 8), :] = plane[x] + add
    after, before = flat.index((0, 1, 0)), flat.index((0, -1, 0))
    fm[pl.ds(7, 8, stride=8), :] += r0[before, 8:16]
    fm[pl.ds(0, 8, stride=8), :] += r0[after, 8:16]
    fm[pl.ds(1, 8, stride=8), :] += r0[after, 16:24]
    left = jnp.where(
        index8 < 8, low_end, jnp.where(index8 == 8, low_end + own_end, 0.0)
    )
    right = jnp.where((index8 == 1) | (index8 == 2), high_end + own_end, high_end)
    both_ends = jnp.concatenate([left, right], axis=0).astype(bf16)
    hb[0:16] = both_ends
    wrapped = jnp.where(lane8 < 64, pltpu.roll(right, 15, 1), pltpu.roll(left, 7, 1))
    hb[80:96] = jnp.concatenate([fm[pl.ds(56, 8), :], wrapped], axis=0).astype(bf16)
    for m in range(4):
        hb[16 + 16 * m : 32 + 16 * m] = fm[pl.ds(16 * m, 16), :].astype(bf16)

    halo = []
    for n, (dx, dy) in enumerate(HALO):
        start, rows = {2: (80, 16), -2: (0, 32)}.get(dx, (0, 80))
        copy = pltpu.make_async_remote_copy(
            src_ref=hb.at[pl.ds(start, rows)], dst_ref=rh.at[n, pl.ds(0, rows)],
            send_sem=send2.at[n], recv_sem=recv2.at[n],
            device_id=device_at(dx, dy, 0), device_id_type=MESH,
        )
        copy.start()
        halo.append(copy)

    xf[...] = jnp.zeros_like(xf)
    for i in range(SPAN):
        xf[32 * (i + 1) : 32 * (i + 1) + SPAN, 0:SPAN] = kern_ref[i].astype(f32)
    xb = xf[...].astype(bf16)
    eye = (
        lax.broadcasted_iota(jnp.int32, (24, 128), 0)
        == lax.broadcasted_iota(jnp.int32, (24, 128), 1)
    ).astype(f32).astype(bf16)
    blocks = []
    for h in range(2):
        kt = mm_nt(eye, xb[32 * (1 - h) : 32 * (1 - h) + 640])
        blocks += [kt[:, 128 * g : 128 * g + 128] for g in range(5)]
    lhs = jnp.concatenate(blocks, axis=0).astype(bf16)
    drow = lax.broadcasted_iota(jnp.int32, (128, 128), 0)
    dlane = lax.broadcasted_iota(jnp.int32, (128, 128), 1)
    base = (drow >> 6) * 64 + ((drow >> 5) & 1) * 8

    def shifted(n, carry):
        r = jnp.where(n < 10, n, 15)
        y = jnp.where(n < 10, n, -1)
        jy = ((drow & 31) + y) & 31
        target = base + (jy >> 3) * 16 + (jy & 7)
        sel = (dlane == target).astype(f32).astype(bf16)
        out = mm(lhs, sel)
        for h in range(2):
            for g in range(5):
                for c in range(3):
                    at = h * 120 + g * 24 + 8 * c
                    tf[g, pl.ds(h * 384 + 128 * c + r, 8, stride=16), :] = out[at : at + 8]
        return carry

    lax.fori_loop(0, 11, shifted, 0)
    for h in range(2):
        for g in range(5):
            for r in range(10, 15):
                for c in range(3):
                    tf[g, pl.ds(h * 384 + 128 * c + r, 8, stride=16), :] = jnp.zeros((8, 128), f32)
            tb[272 * h : 272 * h + 272, 128 * g : 128 * g + 128] = (
                tf[g, 384 * h : 384 * h + 272, :].astype(bf16)
            )

    def place(ends_bf16, main, xp, b, slots):
        at = xp * 64 + b * 16
        w[at : at + 16, 0:128] = main
        wide = ends_bf16.astype(f32)
        tops = []
        for s in slots:
            lo = pltpu.roll(wide[0:8], (119 - 16 * s) % 128, 1)
            hi = pltpu.roll(wide[8:16], (-1 - 16 * s) % 128, 1)
            tops.append(jnp.where(lane8 < 64, hi, lo))
        w[at : at + 16, 128:256] = jnp.concatenate(tops, axis=0).astype(bf16)

    for m in range(4):
        place(hb[0:16], hb[16 + 16 * m : 32 + 16 * m], 5 + m, 1, (2 * m, 2 * m + 1))
    for n in reversed(range(len(HALO))):
        dx, dy = HALO[n]
        halo[n].wait_recv()
        sx, b = -dx, (1 - dy) % 4
        if sx == 2:
            place(rh[n, 0:16], rh[n, 16:32], 13, b, (0, 1))
        elif sx == -2:
            last = rh[n, 0:16].astype(f32)
            blank = jnp.zeros((8, 128), f32)
            for half in range(2):
                w[16 * b : 16 * b + 16, 128 * half : 128 * half + 128] = jnp.concatenate(
                    [blank, last[8 * half : 8 * half + 8]], axis=0
                ).astype(bf16)
        else:
            for m in range(4):
                place(
                    rh[n, 0:16], rh[n, 16 + 16 * m : 32 + 16 * m],
                    4 * sx + 5 + m, b, (2 * m, 2 * m + 1),
                )

    def convolve(p):
        skip = 272 if p == 0 else 0
        out = mm(tb[skip:544, 0:576], w[64 * p : 64 * p + 576, :])
        for h in range(skip // 272, 2):
            acc = None
            for k in range(SPAN):
                at = 272 * h + 16 * k - skip
                term = out[at : at + 16]
                if k != 8:
                    term = pltpu.roll(term, (8 - k) % 256, 1)
                acc = term if acc is None else acc + term
            main, far = acc[:, 0:128], acc[:, 128:256]
            tail = jnp.where(
                (lane16 == 9) | (lane16 == 10),
                pltpu.roll(far, 9, 1),
                jnp.where(lane16 == 16, pltpu.roll(far, 17, 1), 0.0),
            )
            at = (2 * p + h) * 16
            mh, ml = split(main)
            th, tl = split(tail)
            phh[at : at + 16, 0:128] = mh
            phh[at : at + 16, 128:256] = th
            phl[at : at + 16, 0:128] = ml
            phl[at : at + 16, 128:256] = tl
            if 1 <= p <= 4:
                pot_ref[2 * p + h - 2] = main[0:8]

    def interpolate(t):
        at = (t + 1) * 16
        high = phh[at : at + 64, 0:ZROWS]
        both = jnp.concatenate([high, phl[at : at + 64, 0:ZROWS]], axis=0)
        a = mm(both, zwh[t])
        value = a[:64] + a[64:] + mm(high, zwl[t])
        a = mm(both, zsh[t])
        slope = a[:64] + a[64:] + mm(high, zsl[t])
        fx = fy = fz = None
        for k in range(4):
            v, s = value[16 * k : 16 * k + 16], slope[16 * k : 16 * k + 16]
            wx, sx = xs[k, t : t + 1, :], xs[4 + k, t : t + 1, :]
            ax, ay, az = sx * v, wx * v, wx * s
            fx = ax if fx is None else fx + ax
            fy = ay if fy is None else fy + ay
            fz = az if fz is None else fz + az
        wy, sy = ys[0, t], ys[1, t]
        frc_ref[0, t, 0] = jnp.sum(fx * wy, axis=0, keepdims=True)
        frc_ref[1, t, 0] = -jnp.sum(fy * sy, axis=0, keepdims=True)
        frc_ref[2, t, 0] = -jnp.sum(fz * wy, axis=0, keepdims=True)

    for p in range(6):
        convolve(p)
        if p >= 2:
            interpolate(2 * p - 4)
            interpolate(2 * p - 3)

    for copy in fold:
        copy.wait_send()
    for copy in halo:
        copy.wait_send()


def local(charges, offsets, cells, kernel):
    f32, bf16 = jnp.float32, jnp.bfloat16
    vmem = pl.BlockSpec(memory_space=pltpu.VMEM)
    return pl.pallas_call(
        body,
        out_shape=(
            pltpu.VMEM((CX, CY, CZ), f32),
            pltpu.VMEM((3, TILES, 1, 1, APT), f32),
        ),
        in_specs=[pl.BlockSpec(memory_space=pltpu.HBM)] * 4,
        out_specs=(vmem, vmem),
        scratch_shapes=[
            pltpu.VMEM((TILES, APT), f32),
            pltpu.VMEM((3, TILES, APT), f32),
            pltpu.VMEM((2, TILES, APT), jnp.int32),
            pltpu.VMEM((SPAN, SPAN, SPAN), bf16),
            pltpu.VMEM((2, TILES, 16, APT), f32),
            pltpu.VMEM((8, TILES, APT), f32),
            pltpu.VMEM((ZROWS, 128), f32),
            pltpu.VMEM((TILES, ZROWS, APT), bf16),
            pltpu.VMEM((TILES, ZROWS, APT), bf16),
            pltpu.VMEM((TILES, ZROWS, APT), bf16),
            pltpu.VMEM((TILES, ZROWS, APT), bf16),
            pltpu.VMEM((16 * (CX + 3), 128), f32),
            pltpu.VMEM((16 * (CX + 3), 128), f32),
            pltpu.VMEM((2, 2, 2, 8, 128), f32),
            pltpu.VMEM((8, 24, 128), f32),
            pltpu.VMEM((len(FOLD), 8, 128), f32),
            pltpu.VMEM((8, 24, 128), f32),
            pltpu.VMEM((72, 128), f32),
            pltpu.VMEM((96, 128), bf16),
            pltpu.VMEM((len(HALO), 80, 128), bf16),
            pltpu.VMEM((32 * 21, 128), f32),
            pltpu.VMEM((5, 784, 128), f32),
            pltpu.VMEM((544, 640), bf16),
            pltpu.VMEM((14 * 64, 256), bf16),
            pltpu.VMEM((192, 256), bf16),
            pltpu.VMEM((192, 256), bf16),
            pltpu.SemaphoreType.DMA((4,)),
            pltpu.SemaphoreType.DMA((len(FOLD),)),
            pltpu.SemaphoreType.DMA((len(FOLD),)),
            pltpu.SemaphoreType.DMA((len(HALO),)),
            pltpu.SemaphoreType.DMA((len(HALO),)),
        ],
        compiler_params=pltpu.CompilerParams(
            collective_id=0, has_side_effects=True, vmem_limit_bytes=60 * 1024 * 1024
        ),
    )(charges, offsets, cells, kernel)


def solution(mesh):
    placed = (
        P("gx", "gy", "gz", None),
        P(None, "gx", "gy", "gz", None),
        P(None, "gx", "gy", "gz", None),
        P(),
    )
    return jax.shard_map(
        local,
        mesh=mesh,
        in_specs=placed,
        out_specs=(P("gx", "gy", "gz"), P(None, "gx", "gy", "gz", None)),
        check_vma=False,
    )
```
